256 devices in a mesh: dp: 32 (over x, y, core), tensor: 4 (over z_lo), pre: 2 (over z_hi).
Axes of the slice: x: 4, y: 4, z: 8 (z_hi: 2, z_lo: 4; z = z_hi * 4 + z_lo), core: 2. Of those that a mesh axis runs over, the one named last changes fastest.
Arguments:
- acts: bfloat16 [4096, 8192], P('dp', ('tensor', 'pre')), may hold values from -6 to 6
- grad_out: bfloat16 [4096, 2048], P('dp', ('tensor', 'pre')), may hold values from -0.09375 to 0.09375
- owners: int32 [16, 16], P(None, ('tensor', 'pre')), may hold values from 0 to 31, as said below
- left_stats: float32 [32, 2, 512, 4096], P('dp', None, None, ('tensor', 'pre')), may hold values from -0.12 to 256, as said below
- right_stats: float32 [32, 2, 128, 1024], P('dp', None, None, ('tensor', 'pre')), may hold values from -1.9 to 1024, as said below
Outputs:
- new_left: float32 [32, 2, 512, 4096], P('dp', None, None, ('tensor', 'pre'))
- new_right: float32 [32, 2, 128, 1024], P('dp', None, None, ('tensor', 'pre'))
- update: float32 [8192, 2048], P('dp', ('tensor', 'pre'))
The draws below stay inside these ranges and needn't reach their ends.
Inputs may be any that keep to these rules, and one draw needn't show every extreme that they name: `owners`: within every head group no owner holds more than 2 blocks, and some owner holds exactly 2. `left_stats`: Symmetric, with every diagonal entry larger than the sum of magnitudes of its row's other entries. `right_stats`: Symmetric, with every diagonal entry larger than the sum of magnitudes of its row's other entries.
All inputs are finite; a program needn't handle non-finite values.
Results may differ from the reference program's by a relative error of at most 0.0003.
Values may be sent and summed in bfloat16 or wider, within the bound.
A program may use at most 128 MiB of HBM per device.

```python
import jax
import jax.numpy as jnp
from jax import lax

D = 8192
HD = 128
B = 512
CB = 2
ITERS = 3
TOKENS = 4096
NGROUP = 8
RB = 16
MOST = 2
N_DP = 32


def owner_group(group_key):
    slot_total = N_DP * MOST
    count_blocks = RB * CB
    key_star, key_prio, key_perm = jax.random.split(group_key, 3)
    star_owner = jax.random.randint(key_star, (), 0, N_DP)
    slot_ids = jnp.arange(slot_total, dtype=jnp.int32)
    priority = jax.random.permutation(key_prio, slot_total).astype(jnp.int32)
    priority = jnp.where(slot_ids // MOST == star_owner, slot_ids - slot_total, priority)
    chosen = jnp.argsort(priority, stable=True)[:count_blocks].astype(jnp.int32)
    shuffled = jax.random.permutation(key_perm, count_blocks)
    return (chosen[shuffled] // MOST).astype(jnp.int32).reshape(RB, CB)


def draw_owners(key, part):
    key = jax.random.fold_in(key, 11)
    group_keys = jax.random.split(key, NGROUP)
    tables = jax.vmap(owner_group)(group_keys)
    return jnp.transpose(tables, (1, 0, 2)).reshape(RB, NGROUP * CB).astype(jnp.int32)


def dominant_stats(key, size_n, diag_lo, diag_hi, off_bound):
    key_off, key_diag = jax.random.split(key)
    off_part = jax.random.uniform(key_off, (N_DP, MOST, size_n, NGROUP, size_n), jnp.float32, -off_bound, off_bound)
    symmetric = 0.5 * (off_part + jnp.swapaxes(off_part, 2, 4))
    diagonal = jnp.exp(jax.random.uniform(key_diag, (N_DP, MOST, size_n, NGROUP), jnp.float32, jnp.log(diag_lo), jnp.log(diag_hi)))
    row_ids = jnp.arange(size_n)[:, None, None]
    col_ids = jnp.arange(size_n)[None, None, :]
    on_diag = row_ids == col_ids
    full = jnp.where(on_diag, diagonal[..., None], symmetric)
    return full.reshape(N_DP, MOST, size_n, NGROUP * size_n).astype(jnp.float32)


def draw_left_stats(key, part):
    key = jax.random.fold_in(key, 12)
    return dominant_stats(key, B, 64.0, 256.0, 0.1)


def draw_right_stats(key, part):
    key = jax.random.fold_in(key, 13)
    return dominant_stats(key, HD, 256.0, 1024.0, 1.5)


def shard_levels(key, shape, cuts, low, high):
    def one(position, parts):
        draws = jax.random.uniform(jax.random.fold_in(jax.random.fold_in(key, 6), position), (parts,), jnp.float32, low / len(cuts), high / len(cuts))
        return jnp.repeat(jnp.exp(draws), shape[position] // parts).reshape((-1,) + (1,) * (len(shape) - position - 1))

    gain = one(*cuts[0])
    for cut in cuts[1:]:
        gain = gain * one(*cut)
    return gain


def normal_values(rng, shape, scale, bound, shards=(), kind=jnp.bfloat16):
    drawn = jax.random.normal(rng, shape, jnp.float32) * scale
    if len(shards) > 0:
        drawn = shard_levels(rng, shape, shards, -0.22, 0.18) * drawn
    return jnp.clip(drawn, min=-bound, max=bound).astype(kind)


def setup_inputs(seed: int = 0) -> dict:
    arg_keys = jax.random.split(jax.random.key(seed), 6)
    acts = normal_values(arg_keys[0], (TOKENS, D), 1.0, 6.0, ((0, 32), (1, 8)))
    grad_out = normal_values(arg_keys[1], (TOKENS, NGROUP * CB * HD), TOKENS ** -0.5, 0.09375, ((0, 32), (1, 8)))
    owners = draw_owners(jax.random.fold_in(arg_keys[5], 71), 0)
    left_stats = draw_left_stats(jax.random.fold_in(arg_keys[5], 71), 0)
    right_stats = draw_right_stats(jax.random.fold_in(arg_keys[5], 71), 0)
    return {"acts": acts, "grad_out": grad_out, "owners": owners, "left_stats": left_stats, "right_stats": right_stats}


decay_rate = 0.95
graft_eps = 1e-06

def matmul_hi(left, right):
    return jnp.einsum('...ij,...jk->...ik', left, right, precision=lax.Precision.HIGHEST)

def flip_last(matrix):
    return jnp.swapaxes(matrix, -1, -2)

def inverse_root(matrix):
    mat_order = matrix.shape[-1]
    identity = jnp.eye(mat_order, dtype=jnp.float32)
    frob_norm = jnp.sqrt(lax.optimization_barrier(jnp.sum(matrix * matrix, axis=(-2, -1), keepdims=True)))
    scaling = 2.5 / frob_norm
    power_term = scaling * matrix
    root_term = jnp.sqrt(jnp.sqrt(scaling)) * identity
    for repeat in range(ITERS):
        factor = (5.0 * identity - power_term) * 0.25
        root_term = matmul_hi(root_term, factor)
        square = matmul_hi(factor, factor)
        fourth = matmul_hi(square, square)
        power_term = matmul_hi(fourth, power_term)
    return root_term

def slots_of(owner_of):
    block_ids = jnp.arange(owner_of.shape[0], dtype=jnp.int32)
    same_owner = owner_of[:, None] == owner_of[None, :]
    earlier = block_ids[None, :] < block_ids[:, None]
    return lax.optimization_barrier(jnp.sum((same_owner & earlier).astype(jnp.int32), axis=1)).astype(jnp.int32)

def precondition(blocks, left_new, right_new):
    left_root = inverse_root(left_new)
    right_root = inverse_root(right_new)
    shaped = matmul_hi(matmul_hi(left_root, blocks), right_root)
    grad_mean = lax.optimization_barrier(jnp.mean(blocks * blocks, axis=(-2, -1), keepdims=True))
    shaped_mean = lax.optimization_barrier(jnp.mean(shaped * shaped, axis=(-2, -1), keepdims=True))
    return shaped * jnp.sqrt(grad_mean / (shaped_mean + graft_eps))

def reference(acts, grad_out, owners, left_stats, right_stats):
    count_blocks = RB * CB
    col_width = CB * HD
    new_left = decay_rate * left_stats
    new_right = decay_rate * right_stats
    outputs = []
    for column_group in range(NGROUP):
        cotangent = grad_out[:, column_group * col_width:(column_group + 1) * col_width]
        grads = jnp.dot(acts.T, cotangent, preferred_element_type=jnp.float32)
        blocks = grads.reshape(RB, B, CB, HD).transpose(0, 2, 1, 3).reshape(count_blocks, B, HD)
        owner_of = owners[:, column_group * CB:(column_group + 1) * CB].reshape(count_blocks).astype(jnp.int32)
        slot_of = slots_of(owner_of)
        left_old = left_stats[owner_of, slot_of, :, column_group * B:(column_group + 1) * B]
        right_old = right_stats[owner_of, slot_of, :, column_group * HD:(column_group + 1) * HD]
        left_new = decay_rate * left_old + matmul_hi(blocks, flip_last(blocks))
        right_new = decay_rate * right_old + matmul_hi(flip_last(blocks), blocks)
        new_left = new_left.at[owner_of, slot_of, :, column_group * B:(column_group + 1) * B].set(left_new)
        new_right = new_right.at[owner_of, slot_of, :, column_group * HD:(column_group + 1) * HD].set(right_new)
        shaped = precondition(blocks, left_new, right_new)
        outputs.append(shaped.reshape(RB, CB, B, HD).transpose(0, 2, 1, 3).reshape(D, col_width))
    return (new_left, new_right, jnp.concatenate(outputs, axis=1))
```

```python
import jax
import jax.numpy as jnp
from jax import lax
from jax.experimental import pallas as pl
from jax.experimental.pallas import tpu as pltpu
from jax.sharding import PartitionSpec as P

MESH = pl.DeviceIdType.MESH
N_DP = 32
N_Z = 8
CHUNKS = 4
PER = N_DP // CHUNKS
decay_rate = 0.95
graft_eps = 1e-06


def split(x):
    hi = x.astype(jnp.bfloat16)
    lo = (x - hi.astype(jnp.float32)).astype(jnp.bfloat16)
    return hi, lo


def dot(a, b, dims):
    return lax.dot_general(a, b, (dims, ((), ())), preferred_element_type=jnp.float32)


def mul(a, b, dims=((1,), (0,))):
    return dot(a[0], b[0], dims) + (dot(a[0], b[1], dims) + dot(a[1], b[0], dims))


def eye_of(n):
    rows = lax.broadcasted_iota(jnp.int32, (n, n), 0)
    cols = lax.broadcasted_iota(jnp.int32, (n, n), 1)
    return jnp.where(rows == cols, 1.25, 0.0).astype(jnp.float32)


def total(x):
    return jnp.sum(jnp.sum(x, axis=0, keepdims=True), axis=1, keepdims=True)


def precondition(g, left, right):
    eye_l = eye_of(512)
    eye_r = eye_of(128)
    z_l = 2.5 * lax.rsqrt(total(left * left))
    z_r = 2.5 * lax.rsqrt(total(right * right))

    m = z_l * left
    ms = split(m)
    fs = split(eye_l - 0.25 * m)
    ss = split(mul(fs, fs))
    qs = split(mul(ss, ss))
    m2s = split(mul(qs, ms))

    n = z_r * right
    ns = split(n)
    f = eye_r - 0.25 * n
    es = split(f)
    ts = split(mul(es, es))
    us = split(mul(ts, ts))
    n2 = mul(us, ns)
    n2s = split(n2)
    f2 = split(eye_r - 0.25 * n2)
    r12 = split(mul(es, f2))
    ts = split(mul(f2, f2))
    us = split(mul(ts, ts))
    n3 = mul(us, n2s)
    root_r = split(mul(r12, split(eye_r - 0.25 * n3)))

    v1 = 1.25 * g - 0.25 * mul(ms, split(g))
    f2 = split(eye_l - 0.25 * (m2s[0].astype(jnp.float32) + m2s[1].astype(jnp.float32)))
    s2 = split(mul(f2, f2))
    v2 = 1.25 * v1 - 0.25 * mul(m2s, split(v1))
    w = mul(m2s, split(v2))
    w = mul(s2, split(w))
    w = mul(s2, split(w))
    v3 = 1.25 * v2 - 0.25 * w
    shaped = mul(split(v3), root_r)
    shaped = shaped * (jnp.sqrt(jnp.sqrt(z_l)) * jnp.sqrt(jnp.sqrt(z_r)))
    count = 1.0 / (512 * 128)
    grad_mean = total(g * g) * count
    shaped_mean = total(shaped * shaped) * count
    return shaped * jnp.sqrt(grad_mean / (shaped_mean + graft_eps))


def kernel(
    inv, pos, acts_hbm, go_hbm, left_hbm, right_hbm,
    new_left_hbm, new_right_ref, update_ref,
    acts_v, out_a, a_buf, go_buf, left_v, right_v, nl_v, pieces, outbox, inbox,
    retbox, rinbox, fbox, finbox,
    in_sem, out_sem, a_send, a_recv, go_send, go_recv, fw_send,
    zr_send, zr_recv, zl_send, zl_recv,
    d_send, d_recv, r_send, r_recv, f_send, f_recv,
):
    me = lax.axis_index("dp")
    tensor = lax.axis_index("tensor")
    pre = lax.axis_index("pre")
    z = pre * 4 + tensor
    partner = me + 1 - 2 * (me % 2)

    load_acts = pltpu.make_async_copy(acts_hbm, acts_v, in_sem.at[0])
    load_acts.start()
    load_go = pltpu.make_async_copy(go_hbm, go_buf.at[me], in_sem.at[1])
    load_go.start()
    load_left = pltpu.make_async_copy(left_hbm.at[0], left_v, in_sem.at[2])
    load_left.start()
    load_right = pltpu.make_async_copy(right_hbm.at[0], right_v, in_sem.at[3])
    load_right.start()

    def z_dev(zz):
        zz = lax.rem(zz + N_Z, N_Z)
        return {"tensor": lax.rem(zz, 4), "pre": zz // 4}

    def slice_of(zz):
        zz = lax.rem(zz + N_Z, N_Z)
        return lax.rem(zz, 4) * 2 + zz // 4

    barrier = pltpu.get_barrier_semaphore()

    def greet(i, carry):
        pl.semaphore_signal(
            barrier, inc=1, device_id={"dp": lax.rem(me + i, N_DP)}, device_id_type=MESH
        )
        return carry

    lax.fori_loop(1, N_DP, greet, 0)
    for step in (1, -1):
        pl.semaphore_signal(barrier, inc=1, device_id=z_dev(z + step), device_id_type=MESH)

    load_acts.wait()
    for c in range(8):
        turned = acts_v[:, c * 128 : (c + 1) * 128].T
        for e in range(8):
            row = c * 128 + e * 16
            out_a[(row % 512) // 16, (row // 512) * 16 : (row // 512) * 16 + 16] = turned[
                e * 16 : e * 16 + 16
            ]
    mine = slice_of(z)
    a_buf[mine, me] = out_a[me]

    pl.semaphore_wait(barrier, N_DP + 1)

    def send_a(i, carry):
        peer = lax.rem(me + i, N_DP)
        pltpu.make_async_remote_copy(
            src_ref=out_a.at[peer], dst_ref=a_buf.at[mine, me],
            send_sem=a_send.at[i], recv_sem=a_recv.at[me],
            device_id={"dp": peer}, device_id_type=MESH,
        ).start()
        return carry

    lax.fori_loop(1, N_DP, send_a, 0)

    load_go.wait()

    def go_copy(i):
        peer = lax.rem(me + 2 * i, N_DP)
        return pltpu.make_async_remote_copy(
            src_ref=go_buf.at[me], dst_ref=go_buf.at[me],
            send_sem=go_send.at[i], recv_sem=go_recv.at[me],
            device_id={"dp": peer}, device_id_type=MESH,
        )

    def fw_copy(i, src):
        return pltpu.make_async_remote_copy(
            src_ref=go_buf.at[src], dst_ref=go_buf.at[src],
            send_sem=fw_send.at[i], recv_sem=go_recv.at[src],
            device_id={"dp": partner}, device_id_type=MESH,
        )

    def send_go(i, carry):
        go_copy(i).start()
        return carry

    fw_copy(0, me).start()
    lax.fori_loop(1, N_DP // 2, send_go, 0)

    def ring(step, chunk, way):
        sems = (zr_send, zr_recv) if way == 1 else (zl_send, zl_recv)
        ref = a_buf.at[slice_of(z - way * (step - 1)), pl.ds(chunk * PER, PER)]
        return pltpu.make_async_remote_copy(
            src_ref=ref, dst_ref=ref,
            send_sem=sems[0].at[step - 1, chunk], recv_sem=sems[1].at[step - 1, chunk],
            device_id=z_dev(z + way), device_id_type=MESH,
        )

    def arrived(step, chunk, way):
        sems = zr_recv if way == 1 else zl_recv
        ref = a_buf.at[slice_of(z - way * step), pl.ds(chunk * PER, PER)]
        pltpu.make_async_copy(ref, ref, sems.at[step - 1, chunk]).wait()

    def has(step, chunk, way):
        return step < 4 or (chunk < CHUNKS // 2) == (way == 1)

    def wait_a(i, carry):
        @pl.when(i != me)
        def _():
            ref = a_buf.at[mine, i]
            pltpu.make_async_copy(ref, ref, a_recv.at[i]).wait()

        return carry

    def wait_go(src):
        ref = go_buf.at[src]
        pltpu.make_async_copy(ref, ref, go_recv.at[src]).wait()

    def forward_go(i, carry):
        src = lax.rem(me + 2 * i, N_DP)
        wait_go(src)
        fw_copy(i, src).start()
        return carry

    for step in range(1, 5):
        for chunk in range(CHUNKS):
            if step == 1:
                lax.fori_loop(chunk * PER, (chunk + 1) * PER, wait_a, 0)
            for way in (1, -1):
                if step > 1:
                    arrived(step - 1, chunk, way)
                if has(step, chunk, way):
                    ring(step, chunk, way).start()
        if step == 3:
            lax.fori_loop(1, N_DP // 2, forward_go, 0)

    def wait_partner(i, carry):
        wait_go(2 * i + 1 - lax.rem(me, 2))
        return carry

    lax.fori_loop(0, N_DP // 2, wait_partner, 0)
    for chunk in range(CHUNKS):
        arrived(4, chunk, 1 if chunk < CHUNKS // 2 else -1)

    acc = jnp.zeros((256, 256), jnp.float32)
    for m in range(N_DP // 2):
        lhs = jnp.concatenate(
            [a_buf[:, 2 * m].reshape(256, 128), a_buf[:, 2 * m + 1].reshape(256, 128)], axis=1
        )
        acc = acc + jnp.dot(
            lhs, go_buf[2 * m : 2 * m + 2].reshape(256, 256), preferred_element_type=jnp.float32
        )
    for c in range(2):
        pieces[:, c] = acc[:, c * 128 : (c + 1) * 128].reshape(16, 16, 128)

    def fill(o):
        for s in range(2):
            block = inv[2 * o + s]
            used = jnp.maximum(block, 0)
            value = pieces[used // 2, lax.rem(used, 2)]
            outbox[o, s] = jnp.where(block >= 0, value, 0.0)

    def to_owner(i, carry):
        peer = lax.rem(me + i, N_DP)
        fill(peer)
        pltpu.make_async_remote_copy(
            src_ref=outbox.at[peer], dst_ref=inbox.at[me],
            send_sem=d_send.at[i], recv_sem=d_recv.at[me],
            device_id={"dp": peer}, device_id_type=MESH,
        ).start()
        return carry

    lax.fori_loop(1, N_DP, to_owner, 0)
    fill(me)
    inbox[me] = outbox[me]
    load_left.wait()
    load_right.wait()

    def wait_box(box, sem):
        def one(i, carry):
            @pl.when(i != me)
            def _():
                ref = box.at[i]
                pltpu.make_async_copy(ref, ref, sem.at[i]).wait()

            return carry

        lax.fori_loop(0, N_DP, one, 0)

    def wait_sent(box, sem):
        def one(i, carry):
            ref = box.at[0]
            pltpu.make_async_copy(ref, ref, sem.at[i]).wait()
            return carry

        lax.fori_loop(1, N_DP, one, 0)

    wait_box(inbox, d_recv)

    stores = []
    shaped = []
    for s in range(2):
        g = inbox[:, s].reshape(512, 128)
        gs = split(g)
        nl_v[s] = decay_rate * left_v[s] + mul(gs, gs, ((1,), (1,)))
        store = pltpu.make_async_copy(nl_v.at[s], new_left_hbm.at[0, s], out_sem.at[s])
        store.start()
        stores.append(store)
        new_right_ref[0, s] = decay_rate * right_v[s] + mul(gs, gs, ((0,), (0,)))
    for s in range(2):
        g = inbox[:, s].reshape(512, 128)
        shaped.append(precondition(g, nl_v[s], new_right_ref[0, s]))
    for s in range(2):
        for half in range(2):
            retbox[:, s, half] = shaped[s][half * 256 : (half + 1) * 256].reshape(N_DP, 8, 128)

    def send_back(i, carry):
        peer = lax.rem(me + i, N_DP)
        pltpu.make_async_remote_copy(
            src_ref=retbox.at[peer], dst_ref=rinbox.at[me],
            send_sem=r_send.at[i], recv_sem=r_recv.at[me],
            device_id={"dp": peer}, device_id_type=MESH,
        ).start()
        return carry

    lax.fori_loop(1, N_DP, send_back, 0)
    rinbox[me] = retbox[me]
    wait_box(rinbox, r_recv)

    def pick(d):
        for c in range(2):
            where = pos[(d // 2) * 2 + c]
            fbox[d, c] = rinbox[where // 2, lax.rem(where, 2), lax.rem(d, 2)]

    def to_holder(i, carry):
        peer = lax.rem(me + i, N_DP)
        pick(peer)
        pltpu.make_async_remote_copy(
            src_ref=fbox.at[peer], dst_ref=finbox.at[me],
            send_sem=f_send.at[i], recv_sem=f_recv.at[me],
            device_id={"dp": peer}, device_id_type=MESH,
        ).start()
        return carry

    lax.fori_loop(1, N_DP, to_holder, 0)
    pick(me)
    finbox[me] = fbox[me]

    wait_sent(out_a, a_send)
    wait_sent(outbox, d_send)
    wait_sent(retbox, r_send)
    go_ref = go_buf.at[0]

    def wait_go_sent(i, carry):
        pltpu.make_async_copy(go_ref, go_ref, go_send.at[i]).wait()
        pltpu.make_async_copy(go_ref, go_ref, fw_send.at[i]).wait()
        return carry

    lax.fori_loop(1, N_DP // 2, wait_go_sent, 0)
    pltpu.make_async_copy(go_ref, go_ref, fw_send.at[0]).wait()
    for step in range(1, 5):
        for chunk in range(CHUNKS):
            for way in (1, -1):
                if has(step, chunk, way):
                    ring(step, chunk, way).wait_send()
    for store in stores:
        store.wait()

    wait_box(finbox, f_recv)
    for c in range(2):
        update_ref[:, c * 128 : (c + 1) * 128] = finbox[:, c].reshape(256, 128)
    wait_sent(fbox, f_send)


def tables(owners):
    owner_of = owners.reshape(-1)
    ids = jnp.arange(owner_of.shape[0], dtype=jnp.int32)
    earlier = (owner_of[:, None] == owner_of[None, :]) & (ids[None, :] < ids[:, None])
    pos = owner_of * 2 + jnp.sum(earlier.astype(jnp.int32), axis=1)
    places = jnp.arange(2 * N_DP, dtype=jnp.int32)
    hit = (pos[None, :] == places[:, None]).astype(jnp.int32)
    inv = jnp.sum(hit * (ids[None, :] + 1), axis=1) - 1
    return inv, pos


def on_device(acts, grad_out, owners, left_stats, right_stats):
    inv, pos = tables(owners)
    f32, bf16 = jnp.float32, jnp.bfloat16
    dma = pltpu.SemaphoreType.DMA
    vmem = pl.BlockSpec(memory_space=pltpu.VMEM)
    smem = pl.BlockSpec(memory_space=pltpu.SMEM)
    hbm = pl.BlockSpec(memory_space=pl.ANY)
    return pl.pallas_call(
        kernel,
        name="shampoo",
        out_shape=(
            jax.ShapeDtypeStruct(left_stats.shape, f32),
            jax.ShapeDtypeStruct(right_stats.shape, f32),
            jax.ShapeDtypeStruct((256, 256), f32),
        ),
        in_specs=[smem, smem, hbm, hbm, hbm, hbm],
        out_specs=(hbm, vmem, vmem),
        scratch_shapes=[
            pltpu.VMEM((128, 1024), bf16),
            pltpu.VMEM((N_DP, 32, 128), bf16),
            pltpu.VMEM((N_Z, N_DP, 32, 128), bf16),
            pltpu.VMEM((N_DP, 128, 256), bf16),
            pltpu.VMEM((2, 512, 512), f32),
            pltpu.VMEM((2, 128, 128), f32),
            pltpu.VMEM((2, 512, 512), f32),
            pltpu.VMEM((16, 2, 16, 128), f32),
            pltpu.VMEM((N_DP, 2, 16, 128), f32),
            pltpu.VMEM((N_DP, 2, 16, 128), f32),
            pltpu.VMEM((N_DP, 2, 2, 8, 128), f32),
            pltpu.VMEM((N_DP, 2, 2, 8, 128), f32),
            pltpu.VMEM((N_DP, 2, 8, 128), f32),
            pltpu.VMEM((N_DP, 2, 8, 128), f32),
            dma((4,)), dma((2,)),
            dma((N_DP,)), dma((N_DP,)),
            dma((N_DP // 2,)), dma((N_DP,)), dma((N_DP // 2,)),
            dma((4, CHUNKS)), dma((4, CHUNKS)), dma((4, CHUNKS)), dma((4, CHUNKS)),
            dma((N_DP,)), dma((N_DP,)),
            dma((N_DP,)), dma((N_DP,)),
            dma((N_DP,)), dma((N_DP,)),
        ],
        compiler_params=pltpu.CompilerParams(
            collective_id=0, has_side_effects=True, vmem_limit_bytes=48 << 20
        ),
    )(inv, pos, acts, grad_out, left_stats, right_stats)


def solution(mesh):
    in_specs = (
        P("dp", ("tensor", "pre")),
        P("dp", ("tensor", "pre")),
        P(None, ("tensor", "pre")),
        P("dp", None, None, ("tensor", "pre")),
        P("dp", None, None, ("tensor", "pre")),
    )
    out_specs = (
        P("dp", None, None, ("tensor", "pre")),
        P("dp", None, None, ("tensor", "pre")),
        P("dp", ("tensor", "pre")),
    )
    return jax.shard_map(
        on_device, mesh=mesh, in_specs=in_specs, out_specs=out_specs, check_vma=False
    )
```

```python
import jax
import jax.numpy as jnp
from jax import lax
from jax.experimental import pallas as pl
from jax.experimental.pallas import tpu as pltpu
from jax.sharding import PartitionSpec as P

MESH = pl.DeviceIdType.MESH
N_DP = 32
HALF = 16
N_Z = 8
CHUNKS = 4
PER = N_DP // CHUNKS
decay_rate = 0.95
graft_eps = 1e-06


def split(x):
    hi = x.astype(jnp.bfloat16)
    lo = (x - hi.astype(jnp.float32)).astype(jnp.bfloat16)
    return hi, lo


def dot(a, b, dims):
    return lax.dot_general(a, b, (dims, ((), ())), preferred_element_type=jnp.float32)


def mul(a, b, dims=((1,), (0,))):
    return dot(a[0], b[0], dims) + (dot(a[0], b[1], dims) + dot(a[1], b[0], dims))


def eye_of(n):
    rows = lax.broadcasted_iota(jnp.int32, (n, n), 0)
    cols = lax.broadcasted_iota(jnp.int32, (n, n), 1)
    return jnp.where(rows == cols, 1.25, 0.0).astype(jnp.float32)


def total(x):
    return jnp.sum(jnp.sum(x, axis=0, keepdims=True), axis=1, keepdims=True)


def right_steps(right, z_r, out):
    eye = eye_of(128)

    def first():
        n = z_r * right
        out["n"] = split(n)
        out["f1"] = split(eye - 0.25 * n)
        out["s"] = split(mul(out["f1"], out["f1"]))

    def fourth():
        out["q"] = split(mul(out["s"], out["s"]))

    def second():
        n = mul(out["q"], out["n"])
        out["n"] = split(n)
        out["f2"] = split(eye - 0.25 * n)

    def both():
        out["f12"] = split(mul(out["f1"], out["f2"]))
        out["s"] = split(mul(out["f2"], out["f2"]))

    def third():
        out["f3"] = split(eye - 0.25 * mul(out["q"], out["n"]))

    def last():
        out["root"] = split(mul(out["f12"], out["f3"]))

    return [first, fourth, second, both, fourth, third, last]


def precondition(g, left, right):
    eye = eye_of(512)
    z_l = 2.5 * lax.rsqrt(total(left * left))
    z_r = 2.5 * lax.rsqrt(total(right * right))
    made = {}
    steps = right_steps(right, z_r, made)

    def step():
        if steps:
            steps.pop(0)()

    m = z_l * left
    ms = split(m)
    fs = split(eye - 0.25 * m)
    step()
    gt = g.T
    ss = split(mul(fs, fs))
    step()
    v1 = 1.25 * gt - 0.25 * mul(split(gt), ms)
    qs = split(mul(ss, ss))
    step()
    m2s = split(mul(qs, ms))
    step()
    v2 = 1.25 * v1 - 0.25 * mul(split(v1), m2s)
    step()
    w = mul(split(v2), m2s)
    step()
    for _ in range(4):
        w = 1.25 * w - 0.25 * mul(split(w), m2s)
        step()
    v3 = 1.25 * v2 - 0.25 * w
    shaped = mul(made["root"], split(v3)).T
    shaped = shaped * (jnp.sqrt(jnp.sqrt(z_l)) * jnp.sqrt(jnp.sqrt(z_r)))
    count = 1.0 / (512 * 128)
    grad_mean = total(g * g) * count
    shaped_mean = total(shaped * shaped) * count
    return shaped * jnp.sqrt(grad_mean / (shaped_mean + graft_eps))


def kernel(
    inv, pos, acts_hbm, go_hbm, left_hbm, right_hbm,
    nl_out, nr_out, finbox,
    acts_v, out_a, a_buf, go_buf, left_v, right_v, nl_v, nr_v, pieces, outbox, inbox,
    retbox, rinbox, fbox,
    in_sem, out_sem, a_send, a_recv, go_send, go_recv,
    zr_send, zr_recv, zl_send, zl_recv,
    d_send, d_recv, r_send, r_recv, f_send, f_recv,
):
    me = lax.axis_index("dp")
    tensor = lax.axis_index("tensor")
    pre = lax.axis_index("pre")
    z = pre * 4 + tensor
    odd = lax.rem(me, 2)
    partner = me + 1 - 2 * odd

    load_acts = pltpu.make_async_copy(acts_hbm, acts_v, in_sem.at[0])
    load_acts.start()
    load_go = pltpu.make_async_copy(go_hbm, go_buf.at[0, 0], in_sem.at[1])
    load_go.start()
    load_left = pltpu.make_async_copy(left_hbm.at[0], left_v, in_sem.at[2])
    load_left.start()
    load_right = pltpu.make_async_copy(right_hbm.at[0], right_v, in_sem.at[3])
    load_right.start()

    def z_dev(zz):
        zz = lax.rem(zz + N_Z, N_Z)
        return {"tensor": lax.rem(zz, 4), "pre": zz // 4}

    def slice_of(zz):
        zz = lax.rem(zz + N_Z, N_Z)
        return lax.rem(zz, 4) * 2 + zz // 4

    def wait_for(ref, sem):
        pltpu.make_async_copy(ref, ref, sem).wait()

    def to_plane(begin, make):
        def one(i, carry):
            make(i, lax.rem(me + i, N_DP)).start()
            return carry

        lax.fori_loop(begin, N_DP, one, 0)

    barrier = pltpu.get_barrier_semaphore()

    def greet(i, carry):
        pl.semaphore_signal(
            barrier, inc=1, device_id={"dp": lax.rem(me + i, N_DP)}, device_id_type=MESH
        )
        return carry

    lax.fori_loop(1, N_DP, greet, 0)
    for step in (1, -1):
        pl.semaphore_signal(barrier, inc=1, device_id=z_dev(z + step), device_id_type=MESH)

    load_acts.wait()
    for c in range(8):
        turned = acts_v[:, c * 128 : (c + 1) * 128].T
        for e in range(8):
            row = c * 128 + e * 16
            out_a[(row % 512) // 16, (row // 512) * 16 : (row // 512) * 16 + 16] = turned[
                e * 16 : e * 16 + 16
            ]
    mine = slice_of(z)
    pltpu.make_async_copy(out_a.at[me], a_buf.at[mine, 0], a_recv.at[0]).start()

    pl.semaphore_wait(barrier, N_DP + 1)

    to_plane(1, lambda i, peer: pltpu.make_async_remote_copy(
        src_ref=out_a.at[peer], dst_ref=a_buf.at[mine, i],
        send_sem=a_send.at[0], recv_sem=a_recv.at[i // PER],
        device_id={"dp": peer}, device_id_type=MESH,
    ))
    load_go.wait()

    def send_go(j, carry):
        pltpu.make_async_remote_copy(
            src_ref=go_buf.at[0, 0], dst_ref=go_buf.at[0, j],
            send_sem=go_send.at[0], recv_sem=go_recv.at[0],
            device_id={"dp": lax.rem(me + 2 * j, N_DP)}, device_id_type=MESH,
        ).start()
        return carry

    lax.fori_loop(1, HALF, send_go, 0)

    def ring(step, chunk, way):
        sems = (zr_send, zr_recv) if way == 1 else (zl_send, zl_recv)
        ref = a_buf.at[slice_of(z - way * (step - 1)), pl.ds(chunk * PER, PER)]
        return pltpu.make_async_remote_copy(
            src_ref=ref, dst_ref=ref,
            send_sem=sems[0].at[step - 1, chunk], recv_sem=sems[1].at[step - 1, chunk],
            device_id=z_dev(z + way), device_id_type=MESH,
        )

    def arrived(step, chunk, way):
        sems = zr_recv if way == 1 else zl_recv
        wait_for(a_buf.at[slice_of(z - way * step), pl.ds(chunk * PER, PER)], sems.at[step - 1, chunk])

    def has(step, chunk, way):
        return step < 4 or (chunk < CHUNKS // 2) == (way == 1)

    for step in range(1, 5):
        for chunk in range(CHUNKS):
            if step == 1:
                wait_for(a_buf.at[mine, pl.ds(chunk * PER, PER)], a_recv.at[chunk])
            for way in (1, -1):
                if step > 1:
                    arrived(step - 1, chunk, way)
                if has(step, chunk, way):
                    ring(step, chunk, way).start()
        if step == 3:
            wait_for(go_buf.at[0, pl.ds(1, HALF - 1)], go_recv.at[0])
            for src, dst in (
                (go_buf.at[0, pl.ds(odd, HALF - 1)], go_buf.at[1, pl.ds(0, HALF - 1)]),
                (go_buf.at[0, (HALF - 1) * (1 - odd)], go_buf.at[1, HALF - 1]),
            ):
                pltpu.make_async_remote_copy(
                    src_ref=src, dst_ref=dst, send_sem=go_send.at[1], recv_sem=go_recv.at[1],
                    device_id={"dp": partner}, device_id_type=MESH,
                ).start()

    wait_for(out_a.at[pl.ds(0, N_DP - 1)], a_send.at[0])
    wait_for(go_buf.at[0, pl.ds(1, HALF - 1)], go_send.at[0])
    wait_for(go_buf.at[1], go_recv.at[1])
    wait_for(go_buf.at[0], go_send.at[1])
    load_left.wait()
    load_right.wait()
    for chunk in range(CHUNKS):
        arrived(4, chunk, 1 if chunk < CHUNKS // 2 else -1)

    acc = jnp.zeros((256, 256), jnp.float32)
    for m in range(HALF):
        lhs = jnp.concatenate(
            [a_buf[:, 2 * m].reshape(256, 128), a_buf[:, 2 * m + 1].reshape(256, 128)], axis=1
        )
        rhs = jnp.concatenate([go_buf[0, m], go_buf[1, m]], axis=0)
        acc = acc + jnp.dot(lhs, rhs, preferred_element_type=jnp.float32)
    for c in range(2):
        pieces[:, c] = acc[:, c * 128 : (c + 1) * 128].reshape(16, 16, 128)

    for s in range(2):
        def fill(o):
            block = inv[2 * o + s]
            used = jnp.maximum(block, 0)
            value = pieces[used // 2, lax.rem(used, 2)]
            outbox[s, o] = jnp.where(block >= 0, value, 0.0)

        def to_owner(i, peer):
            fill(peer)
            return pltpu.make_async_remote_copy(
                src_ref=outbox.at[s, peer], dst_ref=inbox.at[s, me],
                send_sem=d_send.at[s], recv_sem=d_recv.at[s],
                device_id={"dp": peer}, device_id_type=MESH,
            )

        fill(me)
        pltpu.make_async_copy(outbox.at[s, me], inbox.at[s, me], d_recv.at[s]).start()
        to_plane(1, to_owner)

    for step in range(1, 5):
        for chunk in range(CHUNKS):
            for way in (1, -1):
                if has(step, chunk, way):
                    ring(step, chunk, way).wait_send()

    stores = []
    for s in range(2):
        wait_for(inbox.at[s], d_recv.at[s])
        g = inbox[s].reshape(512, 128)
        gs = split(g)
        nl_v[s] = decay_rate * left_v[s] + mul(gs, gs, ((1,), (1,)))
        nr_v[s] = decay_rate * right_v[s] + mul(gs, gs, ((0,), (0,)))
        for k, (src, dst) in enumerate(((nl_v.at[s], nl_out.at[0, s]), (nr_v.at[s], nr_out.at[0, s]))):
            store = pltpu.make_async_copy(src, dst, out_sem.at[2 * s + k])
            store.start()
            stores.append(store)
        shaped = precondition(g, nl_v[s], nr_v[s])
        for half in range(2):
            retbox[s, :, half] = shaped[half * 256 : (half + 1) * 256].reshape(N_DP, 8, 128)
        pltpu.make_async_copy(retbox.at[s, me], rinbox.at[s, me], r_recv.at[s]).start()
        to_plane(1, lambda i, peer: pltpu.make_async_remote_copy(
            src_ref=retbox.at[s, peer], dst_ref=rinbox.at[s, me],
            send_sem=r_send.at[s], recv_sem=r_recv.at[s],
            device_id={"dp": peer}, device_id_type=MESH,
        ))
    for s in range(2):
        wait_for(outbox.at[s, pl.ds(0, N_DP - 1)], d_send.at[s])
    for s in range(2):
        wait_for(rinbox.at[s], r_recv.at[s])

    def pick(d):
        for c in range(2):
            where = pos[c * 16 + d // 2]
            fbox[d, c] = rinbox[lax.rem(where, 2), where // 2, lax.rem(d, 2)]

    def to_holder(i, peer):
        pick(peer)
        return pltpu.make_async_remote_copy(
            src_ref=fbox.at[peer], dst_ref=finbox.at[me],
            send_sem=f_send.at[0], recv_sem=f_recv.at[0],
            device_id={"dp": peer}, device_id_type=MESH,
        )

    pick(me)
    pltpu.make_async_copy(fbox.at[me], finbox.at[me], f_recv.at[0]).start()
    to_plane(1, to_holder)

    for s in range(2):
        wait_for(retbox.at[s, pl.ds(0, N_DP - 1)], r_send.at[s])
    for store in stores:
        store.wait()
    wait_for(fbox.at[pl.ds(0, N_DP - 1)], f_send.at[0])
    wait_for(finbox, f_recv.at[0])


def export(nl, nr, box, nl_hbm, nr_hbm, up_hbm, sem):
    pairs = [
        (nl.at[0, 0], nl_hbm.at[0, 0]),
        (nl.at[0, 1], nl_hbm.at[0, 1]),
        (nr, nr_hbm),
        (box.at[:, 0], up_hbm.at[:, :, pl.ds(0, 128)]),
        (box.at[:, 1], up_hbm.at[:, :, pl.ds(128, 128)]),
    ]
    copies = [pltpu.make_async_copy(src, dst, sem.at[i]) for i, (src, dst) in enumerate(pairs)]
    for copy in copies:
        copy.start()
    for copy in copies:
        copy.wait()


def tables(owners):
    owner_of = owners.T.reshape(-1)
    at = jnp.arange(2 * 16, dtype=jnp.int32)
    ids = (at % 16) * 2 + at // 16
    earlier = (owner_of[:, None] == owner_of[None, :]) & (ids[None, :] < ids[:, None])
    pos = owner_of * 2 + jnp.sum(earlier.astype(jnp.int32), axis=1)
    places = jnp.arange(2 * N_DP, dtype=jnp.int32)
    hit = (pos[None, :] == places[:, None]).astype(jnp.int32)
    inv = jnp.sum(hit * (ids[None, :] + 1), axis=1) - 1
    return inv, pos


def on_device(acts, grad_out, owners, left_stats, right_stats):
    inv, pos = tables(owners)
    f32, bf16 = jnp.float32, jnp.bfloat16
    dma = pltpu.SemaphoreType.DMA
    vmem = pl.BlockSpec(memory_space=pltpu.VMEM)
    smem = pl.BlockSpec(memory_space=pltpu.SMEM)
    hbm = pl.BlockSpec(memory_space=pl.ANY)
    far = pl.BlockSpec(memory_space=pltpu.HBM)
    left_out = jax.ShapeDtypeStruct(left_stats.shape, f32)
    right_out = jax.ShapeDtypeStruct(right_stats.shape, f32)
    box = jax.ShapeDtypeStruct((N_DP, 2, 8, 128), f32)
    rows = jax.ShapeDtypeStruct((N_DP, 8, 256), f32)
    results = pl.pallas_call(
        kernel,
        name="shampoo",
        out_shape=(left_out, right_out, box),
        in_specs=[smem, smem, far, far, far, far],
        out_specs=(hbm, hbm, hbm),
        scratch_shapes=[
            pltpu.VMEM((128, 1024), bf16),
            pltpu.VMEM((N_DP, 32, 128), bf16),
            pltpu.VMEM((N_Z, N_DP, 32, 128), bf16),
            pltpu.VMEM((2, HALF, 128, 256), bf16),
            pltpu.VMEM((2, 512, 512), f32),
            pltpu.VMEM((2, 128, 128), f32),
            pltpu.VMEM((2, 512, 512), f32),
            pltpu.VMEM((2, 128, 128), f32),
            pltpu.VMEM((16, 2, 16, 128), f32),
            pltpu.VMEM((2, N_DP, 16, 128), f32),
            pltpu.VMEM((2, N_DP, 16, 128), f32),
            pltpu.VMEM((2, N_DP, 2, 8, 128), f32),
            pltpu.VMEM((2, N_DP, 2, 8, 128), f32),
            pltpu.VMEM((N_DP, 2, 8, 128), f32),
            dma((4,)), dma((4,)),
            dma((1,)), dma((CHUNKS,)),
            dma((2,)), dma((2,)),
            dma((4, CHUNKS)), dma((4, CHUNKS)), dma((4, CHUNKS)), dma((4, CHUNKS)),
            dma((2,)), dma((2,)),
            dma((2,)), dma((2,)),
            dma((1,)), dma((1,)),
        ],
        compiler_params=pltpu.CompilerParams(
            collective_id=0, has_side_effects=True, vmem_limit_bytes=32 << 20
        ),
    )(inv, pos, *(pltpu.with_memory_space_constraint(x, pltpu.HBM) for x in (
        acts, grad_out, left_stats, right_stats
    )))
    new_left, new_right, update = pl.pallas_call(
        export,
        name="export",
        out_shape=(left_out, right_out, rows),
        in_specs=[hbm, hbm, hbm],
        out_specs=(far, far, far),
        scratch_shapes=[dma((5,))],
        compiler_params=pltpu.CompilerParams(vmem_limit_bytes=16 << 20),
    )(*results)
    return new_left, new_right, update.reshape(256, 256)


def solution(mesh):
    in_specs = (
        P("dp", ("tensor", "pre")),
        P("dp", ("tensor", "pre")),
        P(None, ("tensor", "pre")),
        P("dp", None, None, ("tensor", "pre")),
        P("dp", None, None, ("tensor", "pre")),
    )
    out_specs = (
        P("dp", None, None, ("tensor", "pre")),
        P("dp", None, None, ("tensor", "pre")),
        P("dp", ("tensor", "pre")),
    )
    return jax.shard_map(
        on_device, mesh=mesh, in_specs=in_specs, out_specs=out_specs, check_vma=False
    )
```

```python
import jax
import jax.numpy as jnp
from jax import lax
from jax.experimental import pallas as pl
from jax.experimental.pallas import tpu as pltpu
from jax.sharding import PartitionSpec as P

MESH = pl.DeviceIdType.MESH
N_DP = 32
HALF = 16
N_Z = 8
CHUNKS = 4
PER = N_DP // CHUNKS
decay_rate = 0.95
graft_eps = 1e-06


def split(x):
    hi = x.astype(jnp.bfloat16)
    lo = (x - hi.astype(jnp.float32)).astype(jnp.bfloat16)
    return hi, lo


def dot(a, b, dims):
    return lax.dot_general(a, b, (dims, ((), ())), preferred_element_type=jnp.float32)


def mul(a, b, dims=((1,), (0,))):
    return dot(a[0], b[0], dims) + (dot(a[0], b[1], dims) + dot(a[1], b[0], dims))


def eye_of(n):
    rows = lax.broadcasted_iota(jnp.int32, (n, n), 0)
    cols = lax.broadcasted_iota(jnp.int32, (n, n), 1)
    return jnp.where(rows == cols, 1.25, 0.0).astype(jnp.float32)


def total(x):
    return jnp.sum(jnp.sum(x, axis=0, keepdims=True), axis=1, keepdims=True)


def right_steps(right, z_r, out):
    eye = eye_of(128)

    def first():
        n = z_r * right
        out["n"] = split(n)
        out["f1"] = split(eye - 0.25 * n)
        out["s"] = split(mul(out["f1"], out["f1"]))

    def fourth():
        out["q"] = split(mul(out["s"], out["s"]))

    def second():
        n = mul(out["q"], out["n"])
        out["n"] = split(n)
        out["f2"] = split(eye - 0.25 * n)

    def both():
        out["f12"] = split(mul(out["f1"], out["f2"]))
        out["s"] = split(mul(out["f2"], out["f2"]))

    def third():
        out["f3"] = split(eye - 0.25 * mul(out["q"], out["n"]))

    def last():
        out["root"] = split(mul(out["f12"], out["f3"]))

    return [first, fourth, second, both, fourth, third, last]


def precondition(g, left, right):
    eye = eye_of(512)
    z_l = 2.5 * lax.rsqrt(total(left * left))
    z_r = 2.5 * lax.rsqrt(total(right * right))
    made = {}
    steps = right_steps(right, z_r, made)

    def step():
        if steps:
            steps.pop(0)()

    m = z_l * left
    ms = split(m)
    fs = split(eye - 0.25 * m)
    step()
    gt = g.T
    ss = split(mul(fs, fs))
    step()
    v1 = 1.25 * gt - 0.25 * mul(split(gt), ms)
    qs = split(mul(ss, ss))
    step()
    m2s = split(mul(qs, ms))
    step()
    v2 = 1.25 * v1 - 0.25 * mul(split(v1), m2s)
    step()
    w = mul(split(v2), m2s)
    step()
    for _ in range(4):
        w = 1.25 * w - 0.25 * mul(split(w), m2s)
        step()
    v3 = 1.25 * v2 - 0.25 * w
    shaped = mul(made["root"], split(v3)).T
    shaped = shaped * (jnp.sqrt(jnp.sqrt(z_l)) * jnp.sqrt(jnp.sqrt(z_r)))
    count = 1.0 / (512 * 128)
    grad_mean = total(g * g) * count
    shaped_mean = total(shaped * shaped) * count
    return shaped * jnp.sqrt(grad_mean / (shaped_mean + graft_eps))


def tables(owners):
    shape = (N_DP, 128)
    sub = lax.broadcasted_iota(jnp.int32, shape, 0)
    lane = lax.broadcasted_iota(jnp.int32, shape, 1)
    across = jnp.full(shape, -1, jnp.int32)
    down = jnp.zeros(shape, jnp.int32)
    for k in range(N_DP):
        owner = owners[k % 2, k // 2]
        across = jnp.where(lane == k, owner, across)
        down = jnp.where(sub == k, owner, down)
    same = across == down
    place = 2 * across[:1] + jnp.sum(
        jnp.where(same & (sub < lane), 1, 0), axis=0, keepdims=True
    )
    place_down = 2 * down + jnp.sum(jnp.where(same & (lane < sub), 1, 0), axis=1, keepdims=True)
    block = jnp.sum(jnp.where(place_down == lane, sub + 1, 0), axis=0, keepdims=True) - 1
    return block, place


def kernel(
    owners_hbm, acts_hbm, go_hbm, left_hbm, right_hbm,
    nl_out, nr_out, finbox,
    owners_s, table_v, table_s, acts_v, out_a, a_buf, go_buf, left_v, right_v, nl_v, nr_v, pieces, outbox, inbox,
    retbox, rinbox, fbox,
    in_sem, out_sem, a_send, a_recv, go_send, go_recv,
    zr_send, zr_recv, zl_send, zl_recv,
    d_send, d_recv, r_send, r_recv, f_send, f_recv,
):
    me = lax.axis_index("dp")
    tensor = lax.axis_index("tensor")
    pre = lax.axis_index("pre")
    z = pre * 4 + tensor
    odd = lax.rem(me, 2)
    partner = me + 1 - 2 * odd
    column = me // PER
    own = lax.rem(me, PER) // 2

    load_owners = pltpu.make_async_copy(owners_hbm, owners_s, in_sem.at[4])
    load_owners.start()
    load_acts = pltpu.make_async_copy(acts_hbm, acts_v, in_sem.at[0])
    load_acts.start()
    load_go = pltpu.make_async_copy(go_hbm, go_buf.at[odd, own], in_sem.at[1])
    load_go.start()
    load_left = pltpu.make_async_copy(left_hbm.at[0], left_v, in_sem.at[2])
    load_left.start()
    load_right = pltpu.make_async_copy(right_hbm.at[0], right_v, in_sem.at[3])
    load_right.start()

    def z_dev(zz):
        zz = lax.rem(zz + N_Z, N_Z)
        return {"tensor": lax.rem(zz, 4), "pre": zz // 4}

    def slice_of(zz):
        zz = lax.rem(zz + N_Z, N_Z)
        return lax.rem(zz, 4) * 2 + zz // 4

    def wait_for(ref, sem):
        pltpu.make_async_copy(ref, ref, sem).wait()

    def to_plane(begin, make):
        def one(i, carry):
            make(i, lax.rem(me + i, N_DP)).start()
            return carry

        lax.fori_loop(begin, N_DP, one, 0)

    barrier = pltpu.get_barrier_semaphore()

    def greet(i, carry):
        pl.semaphore_signal(
            barrier, inc=1, device_id={"dp": lax.rem(me + i, N_DP)}, device_id_type=MESH
        )
        return carry

    lax.fori_loop(1, N_DP, greet, 0)
    for step in (1, -1):
        pl.semaphore_signal(barrier, inc=1, device_id=z_dev(z + step), device_id_type=MESH)

    mine = slice_of(z)
    load_acts.wait()
    for hop in range(CHUNKS):
        goal = lax.rem(column + hop, CHUNKS)
        for part in range(2):
            start = pl.multiple_of((goal + part * CHUNKS) * 128, 128)
            turned = acts_v[:, pl.ds(start, 128)].T
            for e in range(PER):
                out_a[goal * PER + e, part * 16 : part * 16 + 16] = turned[e * 16 : e * 16 + 16]
        if hop == 0:
            pltpu.make_async_copy(
                out_a.at[me], a_buf.at[mine, lax.rem(me, PER)], a_recv.at[0]
            ).start()
            pl.semaphore_wait(barrier, N_DP + 1)

        def send_a(i, carry):
            peer = goal * PER + lax.rem(me + i, PER)
            pltpu.make_async_remote_copy(
                src_ref=out_a.at[peer], dst_ref=a_buf.at[mine, hop * PER + lax.rem(me, PER)],
                send_sem=a_send.at[0], recv_sem=a_recv.at[hop],
                device_id={"dp": peer}, device_id_type=MESH,
            ).start()
            return carry

        lax.fori_loop(1 if hop == 0 else 0, PER, send_a, 0)
    load_go.wait()

    def send_go(j):
        hop, turn = j // 4, j % 4
        peer = lax.rem(column + hop, CHUNKS) * PER + lax.rem(me + 2 * turn, PER)
        pltpu.make_async_remote_copy(
            src_ref=go_buf.at[odd, own], dst_ref=go_buf.at[odd, hop * 4 + own],
            send_sem=go_send.at[0], recv_sem=go_recv.at[0],
            device_id={"dp": peer}, device_id_type=MESH,
        ).start()

    def ring(step, chunk, way):
        sems = (zr_send, zr_recv) if way == 1 else (zl_send, zl_recv)
        ref = a_buf.at[slice_of(z - way * (step - 1)), pl.ds(chunk * PER, PER)]
        return pltpu.make_async_remote_copy(
            src_ref=ref, dst_ref=ref,
            send_sem=sems[0].at[step - 1, chunk], recv_sem=sems[1].at[step - 1, chunk],
            device_id=z_dev(z + way), device_id_type=MESH,
        )

    def arrived(step, chunk, way):
        sems = zr_recv if way == 1 else zl_recv
        wait_for(a_buf.at[slice_of(z - way * step), pl.ds(chunk * PER, PER)], sems.at[step - 1, chunk])

    def has(step, chunk, way):
        return step < 4 or (chunk < CHUNKS // 2) == (way == 1)

    waiting = list(range(1, HALF))
    for step in range(1, 5):
        for chunk in range(CHUNKS):
            if step == 1:
                wait_for(a_buf.at[mine, pl.ds(chunk * PER, PER)], a_recv.at[chunk])
            for way in (1, -1):
                if step > 1:
                    arrived(step - 1, chunk, way)
                if has(step, chunk, way):
                    ring(step, chunk, way).start()
            for _ in range(2):
                if waiting:
                    send_go(waiting.pop(0))

    load_owners.wait()
    block, place = tables(owners_s)
    table_v[0:1] = block
    table_v[1:2] = place
    load_table = pltpu.make_async_copy(table_v, table_s, in_sem.at[5])
    load_table.start()

    wait_for(go_buf.at[0, pl.ds(1, HALF - 1)], go_recv.at[0])
    pltpu.make_async_remote_copy(
        src_ref=go_buf.at[odd], dst_ref=go_buf.at[odd], send_sem=go_send.at[1], recv_sem=go_recv.at[1],
        device_id={"dp": partner}, device_id_type=MESH,
    ).start()
    wait_for(out_a.at[pl.ds(0, N_DP - 1)], a_send.at[0])
    wait_for(go_buf.at[0, pl.ds(1, HALF - 1)], go_send.at[0])
    wait_for(go_buf.at[1], go_recv.at[1])
    wait_for(go_buf.at[0], go_send.at[1])
    load_table.wait()
    load_left.wait()
    load_right.wait()
    for chunk in range(CHUNKS):
        arrived(4, chunk, 1 if chunk < CHUNKS // 2 else -1)

    acc = jnp.zeros((256, 256), jnp.float32)
    for m in range(HALF):
        lhs = jnp.concatenate(
            [a_buf[:, 2 * m].reshape(256, 128), a_buf[:, 2 * m + 1].reshape(256, 128)], axis=1
        )
        rhs = jnp.concatenate([go_buf[0, m], go_buf[1, m]], axis=0)
        acc = acc + jnp.dot(lhs, rhs, preferred_element_type=jnp.float32)
    for c in range(2):
        pieces[:, c] = acc[:, c * 128 : (c + 1) * 128].reshape(16, 16, 128)

    for s in range(2):
        def fill(o):
            block = table_s[0, 2 * o + s]
            used = jnp.maximum(block, 0)
            value = pieces[used // 2, lax.rem(used, 2)]
            outbox[s, o] = jnp.where(block >= 0, value, 0.0)

        def to_owner(i, peer):
            fill(peer)
            return pltpu.make_async_remote_copy(
                src_ref=outbox.at[s, peer], dst_ref=inbox.at[s, me],
                send_sem=d_send.at[s], recv_sem=d_recv.at[s],
                device_id={"dp": peer}, device_id_type=MESH,
            )

        fill(me)
        pltpu.make_async_copy(outbox.at[s, me], inbox.at[s, me], d_recv.at[s]).start()
        to_plane(1, to_owner)

    for step in range(1, 5):
        for chunk in range(CHUNKS):
            for way in (1, -1):
                if has(step, chunk, way):
                    ring(step, chunk, way).wait_send()

    stores = []
    for s in range(2):
        wait_for(inbox.at[s], d_recv.at[s])
        g = inbox[s].reshape(512, 128)
        gs = split(g)
        nl_v[s] = decay_rate * left_v[s] + mul(gs, gs, ((1,), (1,)))
        nr_v[s] = decay_rate * right_v[s] + mul(gs, gs, ((0,), (0,)))
        for k, (src, dst) in enumerate(((nl_v.at[s], nl_out.at[0, s]), (nr_v.at[s], nr_out.at[0, s]))):
            store = pltpu.make_async_copy(src, dst, out_sem.at[2 * s + k])
            store.start()
            stores.append(store)
        shaped = precondition(g, nl_v[s], nr_v[s])
        for half in range(2):
            retbox[s, :, half] = shaped[half * 256 : (half + 1) * 256].reshape(N_DP, 8, 128)
        pltpu.make_async_copy(retbox.at[s, me], rinbox.at[s, me], r_recv.at[s]).start()
        to_plane(1, lambda i, peer: pltpu.make_async_remote_copy(
            src_ref=retbox.at[s, peer], dst_ref=rinbox.at[s, me],
            send_sem=r_send.at[s], recv_sem=r_recv.at[s],
            device_id={"dp": peer}, device_id_type=MESH,
        ))
    for s in range(2):
        wait_for(outbox.at[s, pl.ds(0, N_DP - 1)], d_send.at[s])
    for s in range(2):
        wait_for(rinbox.at[s], r_recv.at[s])

    def pick(d):
        for c in range(2):
            where = table_s[1, 2 * (d // 2) + c]
            fbox[d, c] = rinbox[lax.rem(where, 2), where // 2, lax.rem(d, 2)]

    def to_holder(i, peer):
        pick(peer)
        return pltpu.make_async_remote_copy(
            src_ref=fbox.at[peer], dst_ref=finbox.at[me],
            send_sem=f_send.at[0], recv_sem=f_recv.at[0],
            device_id={"dp": peer}, device_id_type=MESH,
        )

    pick(me)
    pltpu.make_async_copy(fbox.at[me], finbox.at[me], f_recv.at[0]).start()
    to_plane(1, to_holder)

    for s in range(2):
        wait_for(retbox.at[s, pl.ds(0, N_DP - 1)], r_send.at[s])
    for store in stores:
        store.wait()
    wait_for(fbox.at[pl.ds(0, N_DP - 1)], f_send.at[0])
    wait_for(finbox, f_recv.at[0])


def export(nl, nr, box, nl_hbm, nr_hbm, up_hbm, sem):
    pairs = [
        (nl.at[0, 0], nl_hbm.at[0, 0]),
        (nl.at[0, 1], nl_hbm.at[0, 1]),
        (nr, nr_hbm),
        (box.at[:, 0], up_hbm.at[:, :, pl.ds(0, 128)]),
        (box.at[:, 1], up_hbm.at[:, :, pl.ds(128, 128)]),
    ]
    copies = [pltpu.make_async_copy(src, dst, sem.at[i]) for i, (src, dst) in enumerate(pairs)]
    for copy in copies:
        copy.start()
    for copy in copies:
        copy.wait()


def on_device(acts, grad_out, owners, left_stats, right_stats):
    f32, bf16 = jnp.float32, jnp.bfloat16
    dma = pltpu.SemaphoreType.DMA
    vmem = pl.BlockSpec(memory_space=pltpu.VMEM)
    hbm = pl.BlockSpec(memory_space=pl.ANY)
    far = pl.BlockSpec(memory_space=pltpu.HBM)
    left_out = jax.ShapeDtypeStruct(left_stats.shape, f32)
    right_out = jax.ShapeDtypeStruct(right_stats.shape, f32)
    box = jax.ShapeDtypeStruct((N_DP, 2, 8, 128), f32)
    rows = jax.ShapeDtypeStruct((N_DP, 8, 256), f32)
    results = pl.pallas_call(
        kernel,
        name="shampoo",
        out_shape=(left_out, right_out, box),
        in_specs=[far, far, far, far, far],
        out_specs=(hbm, hbm, hbm),
        scratch_shapes=[
            pltpu.SMEM((2, 16), jnp.int32),
            pltpu.VMEM((8, 128), jnp.int32),
            pltpu.SMEM((8, 128), jnp.int32),
            pltpu.VMEM((128, 1024), bf16),
            pltpu.VMEM((N_DP, 32, 128), bf16),
            pltpu.VMEM((N_Z, N_DP, 32, 128), bf16),
            pltpu.VMEM((2, HALF, 128, 256), bf16),
            pltpu.VMEM((2, 512, 512), f32),
            pltpu.VMEM((2, 128, 128), f32),
            pltpu.VMEM((2, 512, 512), f32),
            pltpu.VMEM((2, 128, 128), f32),
            pltpu.VMEM((16, 2, 16, 128), f32),
            pltpu.VMEM((2, N_DP, 16, 128), f32),
            pltpu.VMEM((2, N_DP, 16, 128), f32),
            pltpu.VMEM((2, N_DP, 2, 8, 128), f32),
            pltpu.VMEM((2, N_DP, 2, 8, 128), f32),
            pltpu.VMEM((N_DP, 2, 8, 128), f32),
            dma((6,)), dma((4,)),
            dma((1,)), dma((CHUNKS,)),
            dma((2,)), dma((2,)),
            dma((4, CHUNKS)), dma((4, CHUNKS)), dma((4, CHUNKS)), dma((4, CHUNKS)),
            dma((2,)), dma((2,)),
            dma((2,)), dma((2,)),
            dma((1,)), dma((1,)),
        ],
        compiler_params=pltpu.CompilerParams(
            collective_id=0, has_side_effects=True, vmem_limit_bytes=32 << 20
        ),
    )(*(pltpu.with_memory_space_constraint(x, pltpu.HBM) for x in (
        owners.T, acts, grad_out, left_stats, right_stats
    )))
    new_left, new_right, update = pl.pallas_call(
        export,
        name="export",
        out_shape=(left_out, right_out, rows),
        in_specs=[hbm, hbm, hbm],
        out_specs=(far, far, far),
        scratch_shapes=[dma((5,))],
        compiler_params=pltpu.CompilerParams(vmem_limit_bytes=16 << 20),
    )(*results)
    return new_left, new_right, update.reshape(256, 256)


def solution(mesh):
    in_specs = (
        P("dp", ("tensor", "pre")),
        P("dp", ("tensor", "pre")),
        P(None, ("tensor", "pre")),
        P("dp", None, None, ("tensor", "pre")),
        P("dp", None, None, ("tensor", "pre")),
    )
    out_specs = (
        P("dp", None, None, ("tensor", "pre")),
        P("dp", None, None, ("tensor", "pre")),
        P("dp", ("tensor", "pre")),
    )
    return jax.shard_map(
        on_device, mesh=mesh, in_specs=in_specs, out_specs=out_specs, check_vma=False
    )
```

```python
import jax
import jax.numpy as jnp
from jax import lax
from jax.experimental import pallas as pl
from jax.experimental.pallas import tpu as pltpu
from jax.sharding import PartitionSpec as P

MESH = pl.DeviceIdType.MESH
N_DP = 32
HALF = 16
N_Z = 8
CHUNKS = 4
PER = N_DP // CHUNKS
GO_PACE = (0, 3, 3, 0)
decay_rate = 0.95
graft_eps = 1e-06


def split(x):
    hi = x.astype(jnp.bfloat16)
    lo = (x - hi.astype(jnp.float32)).astype(jnp.bfloat16)
    return hi, lo


def dot(a, b, dims):
    return lax.dot_general(a, b, (dims, ((), ())), preferred_element_type=jnp.float32)


def mul(a, b, dims=((1,), (0,))):
    return dot(a[0], b[0], dims) + (dot(a[0], b[1], dims) + dot(a[1], b[0], dims))


def eye_of(n):
    rows = lax.broadcasted_iota(jnp.int32, (n, n), 0)
    cols = lax.broadcasted_iota(jnp.int32, (n, n), 1)
    return jnp.where(rows == cols, 1.25, 0.0).astype(jnp.float32)


def total(x):
    return jnp.sum(jnp.sum(x, axis=0, keepdims=True), axis=1, keepdims=True)


def right_steps(right, z_r, out):
    eye = eye_of(128)

    def first():
        n = z_r * right
        out["n"] = split(n)
        out["f1"] = split(eye - 0.25 * n)
        out["s"] = split(mul(out["f1"], out["f1"]))

    def fourth():
        out["q"] = split(mul(out["s"], out["s"]))

    def second():
        n = mul(out["q"], out["n"])
        out["n"] = split(n)
        out["f2"] = split(eye - 0.25 * n)

    def both():
        out["f12"] = split(mul(out["f1"], out["f2"]))
        out["s"] = split(mul(out["f2"], out["f2"]))

    def third():
        out["f3"] = split(eye - 0.25 * mul(out["q"], out["n"]))

    def last():
        out["root"] = split(mul(out["f12"], out["f3"]))

    return [first, fourth, second, both, fourth, third, last]


def precondition(g, left, right):
    eye = eye_of(512)
    z_l = 2.5 * lax.rsqrt(total(left * left))
    z_r = 2.5 * lax.rsqrt(total(right * right))
    made = {}
    steps = right_steps(right, z_r, made)

    def step():
        if steps:
            steps.pop(0)()

    m = z_l * left
    ms = split(m)
    fs = split(eye - 0.25 * m)
    step()
    gt = g.T
    ss = split(mul(fs, fs))
    step()
    v1 = 1.25 * gt - 0.25 * mul(split(gt), ms)
    qs = split(mul(ss, ss))
    step()
    m2s = split(mul(qs, ms))
    step()
    v2 = 1.25 * v1 - 0.25 * mul(split(v1), m2s)
    step()
    w = mul(split(v2), m2s)
    step()
    for _ in range(4):
        w = 1.25 * w - 0.25 * mul(split(w), m2s)
        step()
    v3 = 1.25 * v2 - 0.25 * w
    shaped = mul(made["root"], split(v3)).T
    shaped = shaped * (jnp.sqrt(jnp.sqrt(z_l)) * jnp.sqrt(jnp.sqrt(z_r)))
    count = 1.0 / (512 * 128)
    grad_mean = total(g * g) * count
    shaped_mean = total(shaped * shaped) * count
    return shaped * jnp.sqrt(grad_mean / (shaped_mean + graft_eps))


def tables(owners):
    shape = (N_DP, 128)
    sub = lax.broadcasted_iota(jnp.int32, shape, 0)
    lane = lax.broadcasted_iota(jnp.int32, shape, 1)
    across = jnp.full(shape, -1, jnp.int32)
    down = jnp.zeros(shape, jnp.int32)
    for k in range(N_DP):
        owner = owners[k % 2, k // 2]
        across = jnp.where(lane == k, owner, across)
        down = jnp.where(sub == k, owner, down)
    same = across == down
    place = 2 * across[:1] + jnp.sum(
        jnp.where(same & (sub < lane), 1, 0), axis=0, keepdims=True
    )
    place_down = 2 * down + jnp.sum(jnp.where(same & (lane < sub), 1, 0), axis=1, keepdims=True)
    block = jnp.sum(jnp.where(place_down == lane, sub + 1, 0), axis=0, keepdims=True) - 1
    return block, place


def kernel(
    owners_hbm, acts_hbm, go_hbm, left_hbm, right_hbm,
    nl_out, nr_out, up_box,
    owners_s, table_v, table_s, acts_v, out_a, a_buf, go_buf, left_v, right_v,
    sq, sf, rq, rf, tq, tf, uq, uf, old_left, old_right, pieces, gbox, outbox, inbox, half_v,
    in_sem, a_send, a_recv, go_send, go_recv,
    zr_send, zr_recv, zl_send, zl_recv,
    p_send, p_recv, g_send, g_recv, d_send, d_recv, x_send, x_recv,
):
    me = lax.axis_index("dp")
    tensor = lax.axis_index("tensor")
    pre = lax.axis_index("pre")
    z = pre * 4 + tensor
    odd = lax.rem(me, 2)
    partner = me + 1 - 2 * odd
    column = me // PER
    own = lax.rem(me, PER) // 2

    load_owners = pltpu.make_async_copy(owners_hbm, owners_s, in_sem.at[4])
    load_owners.start()
    load_acts = pltpu.make_async_copy(acts_hbm, acts_v, in_sem.at[0])
    load_acts.start()
    load_left = pltpu.make_async_copy(left_hbm.at[0], left_v, in_sem.at[2])
    load_left.start()
    load_right = pltpu.make_async_copy(right_hbm.at[0], right_v, in_sem.at[3])
    load_right.start()
    load_go = pltpu.make_async_copy(go_hbm, go_buf.at[odd, own], in_sem.at[1])
    load_go.start()

    def z_dev(zz):
        zz = lax.rem(zz + N_Z, N_Z)
        return {"tensor": lax.rem(zz, 4), "pre": zz // 4}

    def slice_of(zz):
        zz = lax.rem(zz + N_Z, N_Z)
        return lax.rem(zz, 4) * 2 + zz // 4

    def wait_for(ref, sem):
        pltpu.make_async_copy(ref, ref, sem).wait()

    def to_plane(begin, end, make):
        def one(i, carry):
            make(lax.rem(me + i, N_DP))
            return carry

        lax.fori_loop(max(begin, 1), end, one, 0)

    def send(src, dst, sends, recvs, k, peer):
        pltpu.make_async_remote_copy(
            src_ref=src, dst_ref=dst, send_sem=sends.at[k], recv_sem=recvs.at[k],
            device_id={"dp": peer}, device_id_type=MESH,
        ).start()

    def keep(src, dst, recvs, k):
        pltpu.make_async_copy(src, dst, recvs.at[k]).start()

    def wait_sent(box, sends, k):
        wait_for(box.at[pl.ds(0, N_DP - 1)], sends.at[k])

    barrier = pltpu.get_barrier_semaphore()

    def greet(i, carry):
        pl.semaphore_signal(
            barrier, inc=1, device_id={"dp": lax.rem(me + i, N_DP)}, device_id_type=MESH
        )
        return carry

    lax.fori_loop(1, N_DP, greet, 0)
    for step in (1, -1):
        pl.semaphore_signal(barrier, inc=1, device_id=z_dev(z + step), device_id_type=MESH)

    mine = slice_of(z)
    load_acts.wait()
    for hop in range(CHUNKS):
        goal = lax.rem(column + hop, CHUNKS)
        for part in range(2):
            start = pl.multiple_of((goal + part * CHUNKS) * 128, 128)
            turned = acts_v[:, pl.ds(start, 128)].T
            for e in range(PER):
                out_a[goal * PER + e, part * 16 : part * 16 + 16] = turned[e * 16 : e * 16 + 16]
        if hop == 0:
            pltpu.make_async_copy(
                out_a.at[me], a_buf.at[mine, lax.rem(me, PER)], a_recv.at[0]
            ).start()
            pl.semaphore_wait(barrier, N_DP + 1)

        def send_a(i, carry):
            peer = goal * PER + lax.rem(me + i, PER)
            pltpu.make_async_remote_copy(
                src_ref=out_a.at[peer], dst_ref=a_buf.at[mine, hop * PER + lax.rem(me, PER)],
                send_sem=a_send.at[0], recv_sem=a_recv.at[hop],
                device_id={"dp": peer}, device_id_type=MESH,
            ).start()
            return carry

        lax.fori_loop(1 if hop == 0 else 0, PER, send_a, 0)

    load_left.wait()
    load_right.wait()
    for s in range(2):
        top = jnp.max(left_v[s], axis=0, keepdims=True)
        scale = 32767.0 / jnp.maximum(top, 1e-30)
        for a in range(4):
            for i in range(3):
                b = (a + i) % 4
                level = left_v[s, a * 128 : a * 128 + 128, b * 128 : b * 128 + 128]
                level = jnp.round(level * scale[:, b * 128 : b * 128 + 128])
                level = level.astype(jnp.int32).astype(jnp.int16)
                sq[a * 8 : a * 8 + 8, s, i * 16 : i * 16 + 16] = level.reshape(8, 16, 128)
        for j in range(N_DP):
            a = j // 8
            sf[j, s, 0:4] = right_v[s, 4 * j : 4 * j + 4]
            sf[j, s, 4:8] = jnp.broadcast_to(top[:, a * 128 : a * 128 + 128], (4, 128))
    keep(sq.at[me], rq.at[me], p_recv, 0)
    keep(sf.at[me], rf.at[me], p_recv, 1)

    load_owners.wait()
    block, place = tables(owners_s)
    table_v[0:1] = block
    table_v[1:2] = place
    load_table = pltpu.make_async_copy(table_v, table_s, in_sem.at[5])
    load_table.start()

    load_go.wait()

    def send_go(j):
        hop, turn = j // 4, j % 4
        peer = lax.rem(column + hop, CHUNKS) * PER + lax.rem(me + 2 * turn, PER)
        send(go_buf.at[odd, own], go_buf.at[odd, hop * 4 + own], go_send, go_recv, 0, peer)

    def send_old(peer):
        send(sq.at[peer], rq.at[me], p_send, p_recv, 0, peer)
        send(sf.at[peer], rf.at[me], p_send, p_recv, 1, peer)

    def take_share(k):
        where = table_s[1, k]
        tq[k] = rq[where // 2, lax.rem(where, 2)]
        tf[k] = rf[where // 2, lax.rem(where, 2)]

    def send_share(peer):
        take_share(peer)
        send(tq.at[peer], uq.at[me], p_send, p_recv, 2, peer)
        send(tf.at[peer], uf.at[me], p_send, p_recv, 3, peer)

    def ring(step, chunk, way):
        sems = (zr_send, zr_recv) if way == 1 else (zl_send, zl_recv)
        ref = a_buf.at[slice_of(z - way * (step - 1)), pl.ds(chunk * PER, PER)]
        return pltpu.make_async_remote_copy(
            src_ref=ref, dst_ref=ref,
            send_sem=sems[0].at[step - 1, chunk], recv_sem=sems[1].at[step - 1, chunk],
            device_id=z_dev(z + way), device_id_type=MESH,
        )

    def arrived(step, chunk, way):
        sems = zr_recv if way == 1 else zl_recv
        wait_for(a_buf.at[slice_of(z - way * step), pl.ds(chunk * PER, PER)], sems.at[step - 1, chunk])

    def has(step, chunk, way):
        return step < 4 or (chunk < CHUNKS // 2) == (way == 1)

    waiting = list(range(1, HALF))
    for step in range(1, 5):
        for chunk in range(CHUNKS):
            if step == 1:
                wait_for(a_buf.at[mine, pl.ds(chunk * PER, PER)], a_recv.at[chunk])
            for way in (1, -1):
                if step > 1:
                    arrived(step - 1, chunk, way)
                if has(step, chunk, way):
                    ring(step, chunk, way).start()
            if step == 1:
                to_plane(chunk * PER, (chunk + 1) * PER, send_old)
            for _ in range(GO_PACE[step - 1]):
                if waiting:
                    send_go(waiting.pop(0))
            if step == 4:
                if chunk == 0:
                    load_table.wait()
                    wait_for(rq, p_recv.at[0])
                    wait_for(rf, p_recv.at[1])
                    take_share(me)
                    keep(tq.at[me], uq.at[me], p_recv, 2)
                    keep(tf.at[me], uf.at[me], p_recv, 3)
                to_plane(chunk * PER, (chunk + 1) * PER, send_share)

    wait_for(go_buf.at[0, pl.ds(1, HALF - 1)], go_recv.at[0])
    send(go_buf.at[odd], go_buf.at[odd], go_send, go_recv, 1, partner)
    wait_sent(out_a, a_send, 0)
    wait_for(go_buf.at[0, pl.ds(1, HALF - 1)], go_send.at[0])
    wait_for(go_buf.at[1], go_recv.at[1])
    wait_for(go_buf.at[0], go_send.at[1])
    for chunk in range(CHUNKS):
        arrived(4, chunk, 1 if chunk < CHUNKS // 2 else -1)

    acc = jnp.zeros((256, 256), jnp.float32)
    for m in range(HALF):
        lhs = jnp.concatenate(
            [a_buf[:, 2 * m].reshape(256, 128), a_buf[:, 2 * m + 1].reshape(256, 128)], axis=1
        )
        rhs = jnp.concatenate([go_buf[0, m], go_buf[1, m]], axis=0)
        acc = acc + jnp.dot(lhs, rhs, preferred_element_type=jnp.float32)
    for c in range(2):
        pieces[:, c] = acc[:, c * 128 : (c + 1) * 128].reshape(16, 16, 128)

    keep(pieces.at[me // 2, odd], gbox.at[me], g_recv, 0)
    to_plane(1, N_DP, lambda peer: send(
        pieces.at[peer // 2, lax.rem(peer, 2)], gbox.at[me], g_send, g_recv, 0, peer
    ))

    def fill(o):
        for s in range(2):
            index = table_s[0, 2 * o + s]
            used = jnp.maximum(index, 0)
            value = pieces[used // 2, lax.rem(used, 2)]
            outbox[o, s] = jnp.where(index >= 0, value, 0.0)

    def to_owner(peer):
        fill(peer)
        send(outbox.at[peer], inbox.at[me], d_send, d_recv, 0, peer)

    to_plane(1, N_DP, to_owner)
    fill(me)
    keep(outbox.at[me], inbox.at[me], d_recv, 0)

    wait_for(uq, p_recv.at[2])
    wait_for(uf, p_recv.at[3])
    for a in range(4):
        for i in range(3):
            b = (a + i) % 4
            level = uq[a * 8 : a * 8 + 8, i * 16 : i * 16 + 16].reshape(128, 128)
            level = level.astype(jnp.int32).astype(jnp.float32)
            level = level * (uf[b * 8, 4:5] * (decay_rate / 32767.0))
            old_left[a * 128 : a * 128 + 128, b * 128 : b * 128 + 128] = level
            if i == 1:
                old_left[b * 128 : b * 128 + 128, a * 128 : a * 128 + 128] = level.T
    for j in range(N_DP):
        old_right[4 * j : 4 * j + 4] = decay_rate * uf[j, 0:4]
    wait_sent(sq, p_send, 0)
    wait_sent(sf, p_send, 1)
    wait_sent(tq, p_send, 2)
    wait_sent(tf, p_send, 3)
    for step in range(1, 5):
        for chunk in range(CHUNKS):
            for way in (1, -1):
                if has(step, chunk, way):
                    ring(step, chunk, way).wait_send()

    wait_for(gbox, g_recv.at[0])
    g = gbox[...].reshape(512, 128)
    gs = split(g)
    shaped = precondition(
        g,
        old_left[...] + mul(gs, gs, ((1,), (1,))),
        old_right[...] + mul(gs, gs, ((0,), (0,))),
    )
    for half in range(2):
        half_v[half] = shaped[half * 256 : (half + 1) * 256]
    send(half_v.at[1 - odd], up_box.at[odd], x_send, x_recv, 0, partner)
    keep(half_v.at[odd], up_box.at[odd], x_recv, 1)

    wait_for(inbox, d_recv.at[0])
    for s in range(2):
        gs = split(inbox[:, s].reshape(512, 128))
        nl_out[0, s] = decay_rate * left_v[s] + mul(gs, gs, ((1,), (1,)))
        nr_out[0, s] = decay_rate * right_v[s] + mul(gs, gs, ((0,), (0,)))

    wait_for(pieces.at[pl.ds(0, 15)], g_send.at[0])
    wait_for(pieces.at[15, 0], g_send.at[0])
    wait_sent(outbox, d_send, 0)
    wait_for(half_v.at[0], x_send.at[0])
    wait_for(up_box.at[0], x_recv.at[0])
    wait_for(up_box.at[0], x_recv.at[1])


def export(nl, nr, box, nl_hbm, nr_hbm, up_hbm, sem):
    pairs = [
        (nl.at[0, 0], nl_hbm.at[0, 0]),
        (nl.at[0, 1], nl_hbm.at[0, 1]),
        (nr, nr_hbm),
        (box.at[0], up_hbm.at[:, pl.ds(0, 128)]),
        (box.at[1], up_hbm.at[:, pl.ds(128, 128)]),
    ]
    copies = [pltpu.make_async_copy(src, dst, sem.at[i]) for i, (src, dst) in enumerate(pairs)]
    for copy in copies:
        copy.start()
    for copy in copies:
        copy.wait()


def on_device(acts, grad_out, owners, left_stats, right_stats):
    f32, bf16, i16, i32 = jnp.float32, jnp.bfloat16, jnp.int16, jnp.int32
    dma = pltpu.SemaphoreType.DMA
    vmem = pl.BlockSpec(memory_space=pltpu.VMEM)
    hbm = pl.BlockSpec(memory_space=pl.ANY)
    far = pl.BlockSpec(memory_space=pltpu.HBM)
    left_out = jax.ShapeDtypeStruct(left_stats.shape, f32)
    right_out = jax.ShapeDtypeStruct(right_stats.shape, f32)
    results = pl.pallas_call(
        kernel,
        name="shampoo",
        out_shape=(left_out, right_out, jax.ShapeDtypeStruct((2, 256, 128), f32)),
        in_specs=[far, far, far, far, far],
        out_specs=(vmem, vmem, hbm),
        scratch_shapes=[
            pltpu.SMEM((2, 16), i32),
            pltpu.VMEM((8, 128), i32),
            pltpu.SMEM((8, 128), i32),
            pltpu.VMEM((128, 1024), bf16),
            pltpu.VMEM((N_DP, 32, 128), bf16),
            pltpu.VMEM((N_Z, N_DP, 32, 128), bf16),
            pltpu.VMEM((2, HALF, 128, 256), bf16),
            pltpu.VMEM((2, 512, 512), f32),
            pltpu.VMEM((2, 128, 128), f32),
            pltpu.VMEM((N_DP, 2, 48, 128), i16),
            pltpu.VMEM((N_DP, 2, 8, 128), f32),
            pltpu.VMEM((N_DP, 2, 48, 128), i16),
            pltpu.VMEM((N_DP, 2, 8, 128), f32),
            pltpu.VMEM((N_DP, 48, 128), i16),
            pltpu.VMEM((N_DP, 8, 128), f32),
            pltpu.VMEM((N_DP, 48, 128), i16),
            pltpu.VMEM((N_DP, 8, 128), f32),
            pltpu.VMEM((512, 512), f32),
            pltpu.VMEM((128, 128), f32),
            pltpu.VMEM((16, 2, 16, 128), f32),
            pltpu.VMEM((N_DP, 16, 128), f32),
            pltpu.VMEM((N_DP, 2, 16, 128), f32),
            pltpu.VMEM((N_DP, 2, 16, 128), f32),
            pltpu.VMEM((2, 256, 128), f32),
            dma((6,)),
            dma((1,)), dma((CHUNKS,)),
            dma((2,)), dma((2,)),
            dma((4, CHUNKS)), dma((4, CHUNKS)), dma((4, CHUNKS)), dma((4, CHUNKS)),
            dma((4,)), dma((4,)),
            dma((1,)), dma((1,)),
            dma((1,)), dma((1,)),
            dma((1,)), dma((2,)),
        ],
        compiler_params=pltpu.CompilerParams(
            collective_id=0, has_side_effects=True, vmem_limit_bytes=32 << 20
        ),
    )(*(pltpu.with_memory_space_constraint(x, pltpu.HBM) for x in (
        owners.T, acts, grad_out, left_stats, right_stats
    )))
    return pl.pallas_call(
        export,
        name="export",
        out_shape=(left_out, right_out, jax.ShapeDtypeStruct((256, 256), f32)),
        in_specs=[hbm, hbm, hbm],
        out_specs=(far, far, far),
        scratch_shapes=[dma((5,))],
        compiler_params=pltpu.CompilerParams(vmem_limit_bytes=16 << 20),
    )(*results)


def solution(mesh):
    in_specs = (
        P("dp", ("tensor", "pre")),
        P("dp", ("tensor", "pre")),
        P(None, ("tensor", "pre")),
        P("dp", None, None, ("tensor", "pre")),
        P("dp", None, None, ("tensor", "pre")),
    )
    out_specs = (
        P("dp", None, None, ("tensor", "pre")),
        P("dp", None, None, ("tensor", "pre")),
        P("dp", ("tensor", "pre")),
    )
    return jax.shard_map(
        on_device, mesh=mesh, in_specs=in_specs, out_specs=out_specs, check_vma=False
    )
```

```python
import math

import jax
import jax.numpy as jnp
from jax import lax
from jax.experimental import pallas as pl
from jax.experimental.pallas import tpu as pltpu
from jax.sharding import PartitionSpec as P

MESH = pl.DeviceIdType.MESH
N_DP = 32
HALF = 16
N_Z = 8
CHUNKS = 4
PER = N_DP // CHUNKS
LEVELS = 32760.0
decay_rate = 0.95
graft_eps = 1e-06


def split(x):
    hi = x.astype(jnp.bfloat16)
    lo = (x - hi.astype(jnp.float32)).astype(jnp.bfloat16)
    return hi, lo


def dot(a, b, dims):
    return lax.dot_general(a, b, (dims, ((), ())), preferred_element_type=jnp.float32)


def mul(a, b, dims=((1,), (0,))):
    return dot(a[0], b[0], dims) + (dot(a[0], b[1], dims) + dot(a[1], b[0], dims))


def eye_of(n):
    rows = lax.broadcasted_iota(jnp.int32, (n, n), 0)
    cols = lax.broadcasted_iota(jnp.int32, (n, n), 1)
    return jnp.where(rows == cols, 1.25, 0.0).astype(jnp.float32)


def total(x):
    return jnp.sum(jnp.sum(x, axis=0, keepdims=True), axis=1, keepdims=True)


def right_steps(right, z_r, out):
    eye = eye_of(128)

    def first():
        n = z_r * right
        out["n"] = split(n)
        out["f1"] = split(eye - 0.25 * n)
        out["s"] = split(mul(out["f1"], out["f1"]))

    def fourth():
        out["q"] = split(mul(out["s"], out["s"]))

    def second():
        n = mul(out["q"], out["n"])
        out["n"] = split(n)
        out["f2"] = split(eye - 0.25 * n)

    def both():
        out["f12"] = split(mul(out["f1"], out["f2"]))
        out["s"] = split(mul(out["f2"], out["f2"]))

    def third():
        out["f3"] = split(eye - 0.25 * mul(out["q"], out["n"]))

    def last():
        out["root"] = split(mul(out["f12"], out["f3"]))

    return [first, fourth, second, both, fourth, third, last]


def precondition(g, left, right):
    eye = eye_of(512)
    z_l = 2.5 * lax.rsqrt(total(left * left))
    z_r = 2.5 * lax.rsqrt(total(right * right))
    made = {}
    steps = right_steps(right, z_r, made)

    def step():
        if steps:
            steps.pop(0)()

    m = z_l * left
    ms = split(m)
    fs = split(eye - 0.25 * m)
    step()
    gt = g.T
    ss = split(mul(fs, fs))
    step()
    v1 = 1.25 * gt - 0.25 * mul(split(gt), ms)
    qs = split(mul(ss, ss))
    step()
    m2s = split(mul(qs, ms))
    step()
    v2 = 1.25 * v1 - 0.25 * mul(split(v1), m2s)
    step()
    w = mul(split(v2), m2s)
    step()
    for _ in range(4):
        w = 1.25 * w - 0.25 * mul(split(w), m2s)
        step()
    v3 = 1.25 * v2 - 0.25 * w
    shaped = mul(made["root"], split(v3)).T
    shaped = shaped * (jnp.sqrt(jnp.sqrt(z_l)) * jnp.sqrt(jnp.sqrt(z_r)))
    count = 1.0 / (512 * 128)
    grad_mean = total(g * g) * count
    shaped_mean = total(shaped * shaped) * count
    return shaped * jnp.sqrt(grad_mean / (shaped_mean + graft_eps))


def tables(owners):
    shape = (N_DP, 128)
    sub = lax.broadcasted_iota(jnp.int32, shape, 0)
    lane = lax.broadcasted_iota(jnp.int32, shape, 1)
    across = jnp.full(shape, -1, jnp.int32)
    down = jnp.zeros(shape, jnp.int32)
    for k in range(N_DP):
        owner = owners[k % 2, k // 2]
        across = jnp.where(lane == k, owner, across)
        down = jnp.where(sub == k, owner, down)
    same = across == down
    place = 2 * across[:1] + jnp.sum(
        jnp.where(same & (sub < lane), 1, 0), axis=0, keepdims=True
    )
    place_down = 2 * down + jnp.sum(jnp.where(same & (lane < sub), 1, 0), axis=1, keepdims=True)
    block = jnp.sum(jnp.where(place_down == lane, sub + 1, 0), axis=0, keepdims=True) - 1
    return block, place


def scale_of(stats):
    top = jnp.maximum(jnp.max(stats, axis=0, keepdims=True), 1e-30)
    code = jnp.ceil(jnp.log(top) * (256.0 / math.log(2.0)))
    return code.astype(jnp.int32), LEVELS * jnp.exp2(code * (-1.0 / 256.0))


def unit_of(code):
    return (decay_rate / LEVELS) * jnp.exp2(code.astype(jnp.float32) * (1.0 / 256.0))


def kernel(
    owners_hbm, acts_hbm, go_hbm, left_hbm, right_hbm,
    nl_out, nr_out, up_box,
    owners_s, table_v, table_s, acts_v, out_a, a_buf, go_buf, left_v, right_v,
    sq, rq, tq, uq, old_left, old_right, pieces, gbox, outbox, inbox, half_v,
    in_sem, a_send, a_recv, go_send, go_recv,
    zr_send, zr_recv, zl_send, zl_recv,
    p_send, p_recv, g_send, g_recv, d_send, d_recv, x_send, x_recv,
):
    me = lax.axis_index("dp")
    tensor = lax.axis_index("tensor")
    pre = lax.axis_index("pre")
    z = pre * 4 + tensor
    odd = lax.rem(me, 2)
    partner = me + 1 - 2 * odd
    column = me // PER
    own = lax.rem(me, PER) // 2

    load_owners = pltpu.make_async_copy(owners_hbm, owners_s, in_sem.at[4])
    load_owners.start()
    load_acts = pltpu.make_async_copy(acts_hbm, acts_v, in_sem.at[0])
    load_acts.start()
    load_left = pltpu.make_async_copy(left_hbm.at[0], left_v, in_sem.at[2])
    load_left.start()
    load_right = pltpu.make_async_copy(right_hbm.at[0], right_v, in_sem.at[3])
    load_right.start()
    load_go = pltpu.make_async_copy(go_hbm, go_buf.at[odd, 0, own], in_sem.at[1])
    load_go.start()

    def z_dev(zz):
        zz = lax.rem(zz + N_Z, N_Z)
        return {"tensor": lax.rem(zz, 4), "pre": zz // 4}

    def slice_of(zz):
        zz = lax.rem(zz + N_Z, N_Z)
        return lax.rem(zz, 4) * 2 + zz // 4

    def wait_for(ref, sem):
        pltpu.make_async_copy(ref, ref, sem).wait()

    def to_plane(begin, end, make):
        def one(i, carry):
            make(lax.rem(me + i, N_DP))
            return carry

        lax.fori_loop(max(begin, 1), end, one, 0)

    def send(src, dst, sends, recvs, k, peer):
        pltpu.make_async_remote_copy(
            src_ref=src, dst_ref=dst, send_sem=sends.at[k], recv_sem=recvs.at[k],
            device_id={"dp": peer}, device_id_type=MESH,
        ).start()

    def keep(src, dst, recvs, k):
        pltpu.make_async_copy(src, dst, recvs.at[k]).start()

    def wait_sent(box, sends, k):
        wait_for(box.at[pl.ds(0, N_DP - 1)], sends.at[k])

    barrier = pltpu.get_barrier_semaphore()

    def greet(i, carry):
        pl.semaphore_signal(
            barrier, inc=1, device_id={"dp": lax.rem(me + i, N_DP)}, device_id_type=MESH
        )
        return carry

    lax.fori_loop(1, N_DP, greet, 0)
    for step in (1, -1):
        pl.semaphore_signal(barrier, inc=1, device_id=z_dev(z + step), device_id_type=MESH)

    mine = slice_of(z)
    load_acts.wait()
    for hop in range(CHUNKS):
        goal = lax.rem(column + hop, CHUNKS)
        for part in range(2):
            start = pl.multiple_of((goal + part * CHUNKS) * 128, 128)
            turned = acts_v[:, pl.ds(start, 128)].T
            for e in range(PER):
                out_a[goal * PER + e, part * 16 : part * 16 + 16] = turned[e * 16 : e * 16 + 16]
        if hop == 0:
            pltpu.make_async_copy(
                out_a.at[me], a_buf.at[mine, lax.rem(me, PER)], a_recv.at[0]
            ).start()
            pl.semaphore_wait(barrier, N_DP + 1)

        def send_a(i, carry):
            peer = goal * PER + lax.rem(me + i, PER)
            pltpu.make_async_remote_copy(
                src_ref=out_a.at[peer], dst_ref=a_buf.at[mine, hop * PER + lax.rem(me, PER)],
                send_sem=a_send.at[0], recv_sem=a_recv.at[hop],
                device_id={"dp": peer}, device_id_type=MESH,
            ).start()
            return carry

        lax.fori_loop(1 if hop == 0 else 0, PER, send_a, 0)

    def x_peer(hop):
        return lax.rem(column + hop, CHUNKS) * PER + lax.rem(me, PER)

    def y_peer(hop):
        return column * PER + lax.rem(me + 2 * hop, PER)

    def first_stage(hop):
        near = go_buf.at[odd, 0, own, pl.ds(0, 64)]
        far = go_buf.at[odd, 0, own, pl.ds(64, 64)]
        send(near, go_buf.at[odd, hop, own, pl.ds(0, 64)], go_send, go_recv, 0, x_peer(hop))
        send(far, far, go_send, go_recv, 1, y_peer(hop))

    def second_stage(hop):
        near = go_buf.at[odd, :, own, pl.ds(0, 64)]
        far = go_buf.at[odd, 0, :, pl.ds(64, 64)]
        send(near, near, go_send, go_recv, 2, y_peer(hop))
        send(far, go_buf.at[odd, hop, :, pl.ds(64, 64)], go_send, go_recv, 3, x_peer(hop))

    def wait_first(sems):
        for k in (0, 1):
            wait_for(go_buf.at[0, 0, pl.ds(0, 3), pl.ds(0, 64)], sems.at[k])

    def wait_second(sems):
        for k in (2, 3):
            wait_for(go_buf.at[0, pl.ds(0, 3), :, pl.ds(0, 64)], sems.at[k])

    def send_old(peer):
        send(sq.at[peer], rq.at[me], p_send, p_recv, 0, peer)

    def take_share(k):
        where = table_s[1, k]
        for i in range(3):
            tq[k, i * 16 : i * 16 + 16] = rq[where // 2, lax.rem(where, 2) * 3 + i]
        tq[k, 48:64] = rq[where // 2, 6]

    def send_share(peer):
        take_share(peer)
        send(tq.at[peer], uq.at[me], p_send, p_recv, 1, peer)

    def ring(step, chunk, way):
        sems = (zr_send, zr_recv) if way == 1 else (zl_send, zl_recv)
        ref = a_buf.at[slice_of(z - way * (step - 1)), pl.ds(chunk * PER, PER)]
        return pltpu.make_async_remote_copy(
            src_ref=ref, dst_ref=ref,
            send_sem=sems[0].at[step - 1, chunk], recv_sem=sems[1].at[step - 1, chunk],
            device_id=z_dev(z + way), device_id_type=MESH,
        )

    def arrived(step, chunk, way):
        sems = zr_recv if way == 1 else zl_recv
        wait_for(a_buf.at[slice_of(z - way * step), pl.ds(chunk * PER, PER)], sems.at[step - 1, chunk])

    def has(step, chunk, way):
        return step < 4 or (chunk < CHUNKS // 2) == (way == 1)

    codes_l = []

    def level_left(s):
        if s == 0:
            load_left.wait()
        code, scale = scale_of(left_v[s])
        codes_l.append(code)
        for a in range(4):
            for i in range(3):
                b = (a + i) % 4
                level = left_v[s, a * 128 : a * 128 + 128, b * 128 : b * 128 + 128]
                level = jnp.round(level * scale[:, b * 128 : b * 128 + 128])
                level = level.astype(jnp.int32).astype(jnp.int16)
                sq[a * 8 : a * 8 + 8, s * 3 + i] = level.reshape(8, 16, 128)

    def level_right():
        load_right.wait()
        row = lax.broadcasted_iota(jnp.int32, (8, 128), 0)
        rights, codes_r = [], []
        for s in range(2):
            code, scale = scale_of(right_v[s])
            codes_r.append(code)
            rights.append(jnp.round(right_v[s] * scale).astype(jnp.int32))
        for a in range(4):
            codes = [c[:, a * 128 : a * 128 + 128] for c in codes_l] + codes_r
            low = jnp.where(
                row < 4,
                jnp.where(row < 2, codes[0], codes[1]),
                jnp.where(row < 6, codes[2], codes[3]),
            )
            for j in range(8 * a, 8 * a + 8):
                high = jnp.concatenate([r[4 * j : 4 * j + 4] for r in rights], axis=0)
                sq[j, 6] = jnp.concatenate([high, low], axis=0).astype(jnp.int16)
        keep(sq.at[me], rq.at[me], p_recv, 0)

    def make_tables():
        load_owners.wait()
        block, place = tables(owners_s)
        table_v[0:1] = block
        table_v[1:2] = place
        load_table.start()

    def old(part):
        to_plane(part * PER, (part + 1) * PER, send_old)

    def share(part):
        if part == 0:
            load_table.wait()
            wait_for(rq, p_recv.at[0])
            take_share(me)
            keep(tq.at[me], uq.at[me], p_recv, 1)
        to_plane(part * PER, (part + 1) * PER, send_share)

    load_table = pltpu.make_async_copy(table_v, table_s, in_sem.at[5])
    plan = {
        (1, 0): [load_go.wait, lambda: first_stage(1), lambda: level_left(0)],
        (1, 1): [lambda: first_stage(2), lambda: level_left(1)],
        (1, 2): [lambda: first_stage(3), level_right],
        (1, 3): [lambda: old(0), lambda: old(1)],
        (2, 0): [lambda: old(2), make_tables],
        (2, 1): [lambda: old(3)],
        (2, 2): [lambda: wait_first(go_recv), lambda: second_stage(1)],
        (2, 3): [lambda: second_stage(2)],
        (3, 0): [lambda: second_stage(3)],
        (4, 0): [lambda: share(0)],
        (4, 1): [lambda: share(1)],
        (4, 2): [lambda: share(2)],
        (4, 3): [lambda: share(3)],
    }
    for step in range(1, 5):
        for chunk in range(CHUNKS):
            if step == 1:
                wait_for(a_buf.at[mine, pl.ds(chunk * PER, PER)], a_recv.at[chunk])
            for way in (1, -1):
                if step > 1:
                    arrived(step - 1, chunk, way)
                if has(step, chunk, way):
                    ring(step, chunk, way).start()
            for act in plan.get((step, chunk), ()):
                act()

    wait_second(go_recv)
    send(go_buf.at[odd], go_buf.at[odd], go_send, go_recv, 4, partner)
    wait_sent(out_a, a_send, 0)
    wait_first(go_send)
    wait_second(go_send)
    wait_for(go_buf.at[1], go_recv.at[4])
    wait_for(go_buf.at[0], go_send.at[4])
    for chunk in range(CHUNKS):
        arrived(4, chunk, 1 if chunk < CHUNKS // 2 else -1)

    acc = jnp.zeros((256, 256), jnp.float32)
    for m in range(HALF):
        lhs = jnp.concatenate(
            [a_buf[:, 2 * m].reshape(256, 128), a_buf[:, 2 * m + 1].reshape(256, 128)], axis=1
        )
        rhs = jnp.concatenate([go_buf[0, m // 4, m % 4], go_buf[1, m // 4, m % 4]], axis=0)
        acc = acc + jnp.dot(lhs, rhs, preferred_element_type=jnp.float32)
    for c in range(2):
        pieces[:, c] = acc[:, c * 128 : (c + 1) * 128].reshape(16, 16, 128)

    keep(pieces.at[me // 2, odd], gbox.at[me], g_recv, 0)
    to_plane(1, N_DP, lambda peer: send(
        pieces.at[peer // 2, lax.rem(peer, 2)], gbox.at[me], g_send, g_recv, 0, peer
    ))

    def fill(o):
        for s in range(2):
            index = table_s[0, 2 * o + s]
            used = jnp.maximum(index, 0)
            value = pieces[used // 2, lax.rem(used, 2)]
            outbox[o, s] = jnp.where(index >= 0, value, 0.0)

    def to_owner(peer):
        fill(peer)
        send(outbox.at[peer], inbox.at[me], d_send, d_recv, 0, peer)

    to_plane(1, N_DP, to_owner)
    fill(me)
    keep(outbox.at[me], inbox.at[me], d_recv, 0)

    wait_for(uq, p_recv.at[1])
    second = lax.rem(table_s[1, me], 2) == 1
    for a in range(4):
        for i in range(3):
            b = (a + i) % 4
            codes = uq[b * 8, 48:64].astype(jnp.int32)
            unit = unit_of(jnp.where(second, codes[10:11], codes[8:9]))
            level = uq[a * 8 : a * 8 + 8, i * 16 : i * 16 + 16].reshape(128, 128)
            level = level.astype(jnp.int32).astype(jnp.float32) * unit
            old_left[a * 128 : a * 128 + 128, b * 128 : b * 128 + 128] = level
            if i == 1:
                old_left[b * 128 : b * 128 + 128, a * 128 : a * 128 + 128] = level.T
    codes = uq[0, 48:64].astype(jnp.int32)
    unit = unit_of(jnp.where(second, codes[14:15], codes[12:13]))
    for j in range(N_DP):
        level = uq[j, 48:64].astype(jnp.int32)
        level = jnp.where(second, level[4:8], level[0:4])
        old_right[4 * j : 4 * j + 4] = level.astype(jnp.float32) * unit
    wait_sent(sq, p_send, 0)
    wait_sent(tq, p_send, 1)
    for step in range(1, 5):
        for chunk in range(CHUNKS):
            for way in (1, -1):
                if has(step, chunk, way):
                    ring(step, chunk, way).wait_send()

    wait_for(gbox, g_recv.at[0])
    g = gbox[...].reshape(512, 128)
    gs = split(g)
    shaped = precondition(
        g,
        old_left[...] + mul(gs, gs, ((1,), (1,))),
        old_right[...] + mul(gs, gs, ((0,), (0,))),
    )
    for half in range(2):
        half_v[half] = shaped[half * 256 : (half + 1) * 256]
    send(half_v.at[1 - odd], up_box.at[odd], x_send, x_recv, 0, partner)
    keep(half_v.at[odd], up_box.at[odd], x_recv, 1)

    wait_for(inbox, d_recv.at[0])
    for s in range(2):
        gs = split(inbox[:, s].reshape(512, 128))
        nl_out[0, s] = decay_rate * left_v[s] + mul(gs, gs, ((1,), (1,)))
        nr_out[0, s] = decay_rate * right_v[s] + mul(gs, gs, ((0,), (0,)))

    wait_for(pieces.at[pl.ds(0, 15)], g_send.at[0])
    wait_for(pieces.at[15, 0], g_send.at[0])
    wait_sent(outbox, d_send, 0)
    wait_for(half_v.at[0], x_send.at[0])
    wait_for(up_box.at[0], x_recv.at[0])
    wait_for(up_box.at[0], x_recv.at[1])


def export(nl, nr, box, nl_hbm, nr_hbm, up_hbm, sem):
    pairs = [
        (nl.at[0, 0], nl_hbm.at[0, 0]),
        (nl.at[0, 1], nl_hbm.at[0, 1]),
        (nr, nr_hbm),
        (box.at[0], up_hbm.at[:, pl.ds(0, 128)]),
        (box.at[1], up_hbm.at[:, pl.ds(128, 128)]),
    ]
    copies = [pltpu.make_async_copy(src, dst, sem.at[i]) for i, (src, dst) in enumerate(pairs)]
    for copy in copies:
        copy.start()
    for copy in copies:
        copy.wait()


def on_device(acts, grad_out, owners, left_stats, right_stats):
    f32, bf16, i16, i32 = jnp.float32, jnp.bfloat16, jnp.int16, jnp.int32
    dma = pltpu.SemaphoreType.DMA
    vmem = pl.BlockSpec(memory_space=pltpu.VMEM)
    hbm = pl.BlockSpec(memory_space=pl.ANY)
    far = pl.BlockSpec(memory_space=pltpu.HBM)
    left_out = jax.ShapeDtypeStruct(left_stats.shape, f32)
    right_out = jax.ShapeDtypeStruct(right_stats.shape, f32)
    results = pl.pallas_call(
        kernel,
        name="shampoo",
        out_shape=(left_out, right_out, jax.ShapeDtypeStruct((2, 256, 128), f32)),
        in_specs=[far, far, far, far, far],
        out_specs=(vmem, vmem, hbm),
        scratch_shapes=[
            pltpu.SMEM((2, 16), i32),
            pltpu.VMEM((8, 128), i32),
            pltpu.SMEM((8, 128), i32),
            pltpu.VMEM((128, 1024), bf16),
            pltpu.VMEM((N_DP, 32, 128), bf16),
            pltpu.VMEM((N_Z, N_DP, 32, 128), bf16),
            pltpu.VMEM((2, 4, 4, 128, 256), bf16),
            pltpu.VMEM((2, 512, 512), f32),
            pltpu.VMEM((2, 128, 128), f32),
            pltpu.VMEM((N_DP, 7, 16, 128), i16),
            pltpu.VMEM((N_DP, 7, 16, 128), i16),
            pltpu.VMEM((N_DP, 64, 128), i16),
            pltpu.VMEM((N_DP, 64, 128), i16),
            pltpu.VMEM((512, 512), f32),
            pltpu.VMEM((128, 128), f32),
            pltpu.VMEM((16, 2, 16, 128), f32),
            pltpu.VMEM((N_DP, 16, 128), f32),
            pltpu.VMEM((N_DP, 2, 16, 128), f32),
            pltpu.VMEM((N_DP, 2, 16, 128), f32),
            pltpu.VMEM((2, 256, 128), f32),
            dma((6,)),
            dma((1,)), dma((CHUNKS,)),
            dma((5,)), dma((5,)),
            dma((4, CHUNKS)), dma((4, CHUNKS)), dma((4, CHUNKS)), dma((4, CHUNKS)),
            dma((2,)), dma((2,)),
            dma((1,)), dma((1,)),
            dma((1,)), dma((1,)),
            dma((1,)), dma((2,)),
        ],
        compiler_params=pltpu.CompilerParams(
            collective_id=0, has_side_effects=True, vmem_limit_bytes=32 << 20
        ),
    )(*(pltpu.with_memory_space_constraint(x, pltpu.HBM) for x in (
        owners.T, acts, grad_out, left_stats, right_stats
    )))
    return pl.pallas_call(
        export,
        name="export",
        out_shape=(left_out, right_out, jax.ShapeDtypeStruct((256, 256), f32)),
        in_specs=[hbm, hbm, hbm],
        out_specs=(far, far, far),
        scratch_shapes=[dma((5,))],
        compiler_params=pltpu.CompilerParams(vmem_limit_bytes=16 << 20),
    )(*results)


def solution(mesh):
    in_specs = (
        P("dp", ("tensor", "pre")),
        P("dp", ("tensor", "pre")),
        P(None, ("tensor", "pre")),
        P("dp", None, None, ("tensor", "pre")),
        P("dp", None, None, ("tensor", "pre")),
    )
    out_specs = (
        P("dp", None, None, ("tensor", "pre")),
        P("dp", None, None, ("tensor", "pre")),
        P("dp", ("tensor", "pre")),
    )
    return jax.shard_map(
        on_device, mesh=mesh, in_specs=in_specs, out_specs=out_specs, check_vma=False
    )
```

```python
import math

import jax
import jax.numpy as jnp
from jax import lax
from jax.experimental import pallas as pl
from jax.experimental.pallas import tpu as pltpu
from jax.sharding import PartitionSpec as P

MESH = pl.DeviceIdType.MESH
N_DP = 32
HALF = 16
N_Z = 8
CHUNKS = 4
PER = N_DP // CHUNKS
LEVELS = 32760.0
decay_rate = 0.95
graft_eps = 1e-06


def split(x):
    hi = x.astype(jnp.bfloat16)
    lo = (x - hi.astype(jnp.float32)).astype(jnp.bfloat16)
    return hi, lo


def dot(a, b, dims):
    return lax.dot_general(a, b, (dims, ((), ())), preferred_element_type=jnp.float32)


def mul(a, b, dims=((1,), (0,))):
    return dot(a[0], b[0], dims) + (dot(a[0], b[1], dims) + dot(a[1], b[0], dims))


def eye_of(n):
    rows = lax.broadcasted_iota(jnp.int32, (n, n), 0)
    cols = lax.broadcasted_iota(jnp.int32, (n, n), 1)
    return jnp.where(rows == cols, 1.25, 0.0).astype(jnp.float32)


def total(x):
    return jnp.sum(jnp.sum(x, axis=0, keepdims=True), axis=1, keepdims=True)


def right_steps(right, z_r, out):
    eye = eye_of(128)

    def first():
        n = z_r * right
        out["n"] = split(n)
        out["f1"] = split(eye - 0.25 * n)
        out["s"] = split(mul(out["f1"], out["f1"]))

    def fourth():
        out["q"] = split(mul(out["s"], out["s"]))

    def second():
        n = mul(out["q"], out["n"])
        out["n"] = split(n)
        out["f2"] = split(eye - 0.25 * n)

    def both():
        out["f12"] = split(mul(out["f1"], out["f2"]))
        out["s"] = split(mul(out["f2"], out["f2"]))

    def third():
        out["f3"] = split(eye - 0.25 * mul(out["q"], out["n"]))

    def last():
        out["root"] = split(mul(out["f12"], out["f3"]))

    return [first, fourth, second, both, fourth, third, last]


def precondition(g, left, right):
    eye = eye_of(512)
    z_l = 2.5 * lax.rsqrt(total(left * left))
    z_r = 2.5 * lax.rsqrt(total(right * right))
    made = {}
    steps = right_steps(right, z_r, made)

    def step():
        if steps:
            steps.pop(0)()

    m = z_l * left
    ms = split(m)
    fs = split(eye - 0.25 * m)
    step()
    gt = g.T
    ss = split(mul(fs, fs))
    step()
    v1 = 1.25 * gt - 0.25 * mul(split(gt), ms)
    qs = split(mul(ss, ss))
    step()
    m2s = split(mul(qs, ms))
    step()
    v2 = 1.25 * v1 - 0.25 * mul(split(v1), m2s)
    step()
    w = mul(split(v2), m2s)
    step()
    for _ in range(4):
        w = 1.25 * w - 0.25 * mul(split(w), m2s)
        step()
    v3 = 1.25 * v2 - 0.25 * w
    shaped = mul(made["root"], split(v3)).T
    shaped = shaped * (jnp.sqrt(jnp.sqrt(z_l)) * jnp.sqrt(jnp.sqrt(z_r)))
    count = 1.0 / (512 * 128)
    grad_mean = total(g * g) * count
    shaped_mean = total(shaped * shaped) * count
    return shaped * jnp.sqrt(grad_mean / (shaped_mean + graft_eps))


def tables(owners):
    shape = (N_DP, 128)
    sub = lax.broadcasted_iota(jnp.int32, shape, 0)
    lane = lax.broadcasted_iota(jnp.int32, shape, 1)
    across = jnp.full(shape, -1, jnp.int32)
    down = jnp.zeros(shape, jnp.int32)
    for k in range(N_DP):
        owner = owners[k % 2, k // 2]
        across = jnp.where(lane == k, owner, across)
        down = jnp.where(sub == k, owner, down)
    same = across == down
    place = 2 * across[:1] + jnp.sum(
        jnp.where(same & (sub < lane), 1, 0), axis=0, keepdims=True
    )
    place_down = 2 * down + jnp.sum(jnp.where(same & (lane < sub), 1, 0), axis=1, keepdims=True)
    block = jnp.sum(jnp.where(place_down == lane, sub + 1, 0), axis=0, keepdims=True) - 1
    return block, place


def scale_of(stats):
    top = jnp.maximum(jnp.max(stats, axis=0, keepdims=True), 1e-30)
    code = jnp.ceil(jnp.log(top) * (256.0 / math.log(2.0)))
    return code.astype(jnp.int32), LEVELS * jnp.exp2(code * (-1.0 / 256.0))


def unit_of(code):
    return (decay_rate / LEVELS) * jnp.exp2(code.astype(jnp.float32) * (1.0 / 256.0))


def kernel(
    owners_hbm, acts_hbm, go_hbm, left_hbm, right_hbm,
    nl_out, nr_out, up_box,
    owners_s, table_v, table_s, acts_v, out_a, a_buf, go_buf, left_v, right_v,
    sq, rq, tq, uq, old_left, old_right, pieces, gbox, outbox, inbox, half_v,
    in_sem, a_send, a_recv, go_send, go_recv,
    zr_send, zr_recv, zl_send, zl_recv,
    p_send, p_recv, g_send, g_recv, d_send, d_recv, x_send, x_recv,
):
    me = lax.axis_index("dp")
    tensor = lax.axis_index("tensor")
    pre = lax.axis_index("pre")
    z = pre * 4 + tensor
    odd = lax.rem(me, 2)
    partner = me + 1 - 2 * odd
    column = me // PER
    own = lax.rem(me, PER) // 2

    load_owners = pltpu.make_async_copy(owners_hbm, owners_s, in_sem.at[4])
    load_owners.start()
    load_acts = pltpu.make_async_copy(acts_hbm, acts_v, in_sem.at[0])
    load_acts.start()
    load_left = pltpu.make_async_copy(left_hbm.at[0], left_v, in_sem.at[2])
    load_left.start()
    load_right = pltpu.make_async_copy(right_hbm.at[0], right_v, in_sem.at[3])
    load_right.start()
    load_go = pltpu.make_async_copy(go_hbm, go_buf.at[odd, 0, own], in_sem.at[1])
    load_go.start()

    def z_dev(zz):
        zz = lax.rem(zz + N_Z, N_Z)
        return {"tensor": lax.rem(zz, 4), "pre": zz // 4}

    def slice_of(zz):
        zz = lax.rem(zz + N_Z, N_Z)
        return lax.rem(zz, 4) * 2 + zz // 4

    def wait_for(ref, sem):
        pltpu.make_async_copy(ref, ref, sem).wait()

    def to_plane(begin, end, make):
        def one(i, carry):
            make(lax.rem(me + i, N_DP))
            return carry

        lax.fori_loop(max(begin, 1), end, one, 0)

    def send(src, dst, sends, recvs, k, peer):
        pltpu.make_async_remote_copy(
            src_ref=src, dst_ref=dst, send_sem=sends.at[k], recv_sem=recvs.at[k],
            device_id={"dp": peer}, device_id_type=MESH,
        ).start()

    def keep(src, dst, recvs, k):
        pltpu.make_async_copy(src, dst, recvs.at[k]).start()

    def wait_sent(box, sends, k):
        wait_for(box.at[pl.ds(0, N_DP - 1)], sends.at[k])

    barrier = pltpu.get_barrier_semaphore()

    def greet(i, carry):
        pl.semaphore_signal(
            barrier, inc=1, device_id={"dp": lax.rem(me + i, N_DP)}, device_id_type=MESH
        )
        return carry

    lax.fori_loop(1, N_DP, greet, 0)
    for step in (1, -1):
        pl.semaphore_signal(barrier, inc=1, device_id=z_dev(z + step), device_id_type=MESH)

    mine = slice_of(z)
    load_acts.wait()
    for hop in range(CHUNKS):
        goal = lax.rem(column + hop, CHUNKS)
        for part in range(2):
            start = pl.multiple_of((goal + part * CHUNKS) * 128, 128)
            turned = acts_v[:, pl.ds(start, 128)].T
            for e in range(PER):
                out_a[goal * PER + e, part * 16 : part * 16 + 16] = turned[e * 16 : e * 16 + 16]
        if hop == 0:
            pltpu.make_async_copy(
                out_a.at[me], a_buf.at[mine, lax.rem(me, PER)], a_recv.at[0]
            ).start()
            pl.semaphore_wait(barrier, N_DP + 1)

        def send_a(i, carry):
            peer = goal * PER + lax.rem(me + i, PER)
            pltpu.make_async_remote_copy(
                src_ref=out_a.at[peer], dst_ref=a_buf.at[mine, hop * PER + lax.rem(me, PER)],
                send_sem=a_send.at[0], recv_sem=a_recv.at[hop],
                device_id={"dp": peer}, device_id_type=MESH,
            ).start()
            return carry

        lax.fori_loop(1 if hop == 0 else 0, PER, send_a, 0)

    def x_peer(hop):
        return lax.rem(column + hop, CHUNKS) * PER + lax.rem(me, PER)

    def y_peer(hop):
        return column * PER + lax.rem(me + 2 * hop, PER)

    def first_stage(hop):
        near = go_buf.at[odd, 0, own, pl.ds(0, 64)]
        far = go_buf.at[odd, 0, own, pl.ds(64, 64)]
        send(near, go_buf.at[odd, hop, own, pl.ds(0, 64)], go_send, go_recv, 0, x_peer(hop))
        send(far, far, go_send, go_recv, 1, y_peer(hop))

    def second_stage(hop):
        near = go_buf.at[odd, :, own, pl.ds(0, 64)]
        far = go_buf.at[odd, 0, :, pl.ds(64, 64)]
        send(near, near, go_send, go_recv, 2, y_peer(hop))
        send(far, go_buf.at[odd, hop, :, pl.ds(64, 64)], go_send, go_recv, 3, x_peer(hop))

    def wait_first(sems):
        for k in (0, 1):
            wait_for(go_buf.at[0, 0, pl.ds(0, 3), pl.ds(0, 64)], sems.at[k])

    def wait_second(sems):
        for k in (2, 3):
            wait_for(go_buf.at[0, pl.ds(0, 3), :, pl.ds(0, 64)], sems.at[k])

    def send_old(peer):
        send(sq.at[peer], rq.at[me], p_send, p_recv, 0, peer)

    def take_share(k):
        where = table_s[1, k]
        for i in range(3):
            tq[k, i * 16 : i * 16 + 16] = rq[where // 2, lax.rem(where, 2) * 3 + i]
        tq[k, 48:64] = rq[where // 2, 6]

    def send_share(peer):
        take_share(peer)
        send(tq.at[peer], uq.at[me], p_send, p_recv, 1, peer)

    def ring(step, chunk, way):
        sems = (zr_send, zr_recv) if way == 1 else (zl_send, zl_recv)
        ref = a_buf.at[slice_of(z - way * (step - 1)), pl.ds(chunk * PER, PER)]
        return pltpu.make_async_remote_copy(
            src_ref=ref, dst_ref=ref,
            send_sem=sems[0].at[step - 1, chunk], recv_sem=sems[1].at[step - 1, chunk],
            device_id=z_dev(z + way), device_id_type=MESH,
        )

    def arrived(step, chunk, way):
        sems = zr_recv if way == 1 else zl_recv
        wait_for(a_buf.at[slice_of(z - way * step), pl.ds(chunk * PER, PER)], sems.at[step - 1, chunk])

    def has(step, chunk, way):
        return step < 4 or (chunk < CHUNKS // 2) == (way == 1)

    codes_l = []

    def level_left(s):
        if s == 0:
            load_left.wait()
        code, scale = scale_of(left_v[s])
        codes_l.append(code)
        for a in range(4):
            for i in range(3):
                b = (a + i) % 4
                level = left_v[s, a * 128 : a * 128 + 128, b * 128 : b * 128 + 128]
                level = jnp.round(level * scale[:, b * 128 : b * 128 + 128])
                level = level.astype(jnp.int32).astype(jnp.int16)
                sq[a * 8 : a * 8 + 8, s * 3 + i] = level.reshape(8, 16, 128)

    def level_right():
        load_right.wait()
        row = lax.broadcasted_iota(jnp.int32, (8, 128), 0)
        rights, codes_r = [], []
        for s in range(2):
            code, scale = scale_of(right_v[s])
            codes_r.append(code)
            rights.append(jnp.round(right_v[s] * scale).astype(jnp.int32))
        for a in range(4):
            codes = [c[:, a * 128 : a * 128 + 128] for c in codes_l] + codes_r
            low = jnp.where(
                row < 4,
                jnp.where(row < 2, codes[0], codes[1]),
                jnp.where(row < 6, codes[2], codes[3]),
            )
            for j in range(8 * a, 8 * a + 8):
                high = jnp.concatenate([r[4 * j : 4 * j + 4] for r in rights], axis=0)
                sq[j, 6] = jnp.concatenate([high, low], axis=0).astype(jnp.int16)
        keep(sq.at[me], rq.at[me], p_recv, 0)

    def make_tables():
        load_owners.wait()
        block, place = tables(owners_s)
        table_v[0:1] = block
        table_v[1:2] = place
        load_table.start()

    def old(part):
        to_plane(part * PER, (part + 1) * PER, send_old)

    def share(part):
        if part == 0:
            load_table.wait()
            wait_for(rq, p_recv.at[0])
            take_share(me)
            keep(tq.at[me], uq.at[me], p_recv, 1)
        to_plane(part * PER, (part + 1) * PER, send_share)

    load_table = pltpu.make_async_copy(table_v, table_s, in_sem.at[5])
    plan = {
        (1, 0): [load_go.wait, lambda: first_stage(1), lambda: level_left(0)],
        (1, 1): [lambda: first_stage(2), lambda: level_left(1)],
        (1, 2): [lambda: first_stage(3), level_right],
        (1, 3): [lambda: old(0), lambda: old(1)],
        (2, 0): [lambda: old(2), make_tables],
        (2, 1): [lambda: old(3)],
        (2, 2): [lambda: wait_first(go_recv), lambda: second_stage(1)],
        (2, 3): [lambda: second_stage(2)],
        (3, 0): [lambda: second_stage(3)],
        (4, 0): [lambda: share(0)],
    }
    for step in range(1, 5):
        for chunk in range(CHUNKS):
            if step == 1:
                wait_for(a_buf.at[mine, pl.ds(chunk * PER, PER)], a_recv.at[chunk])
            for way in (1, -1):
                if step > 1:
                    arrived(step - 1, chunk, way)
                if has(step, chunk, way):
                    ring(step, chunk, way).start()
            for act in plan.get((step, chunk), ()):
                act()

    wait_second(go_recv)
    send(go_buf.at[odd], go_buf.at[odd], go_send, go_recv, 4, partner)
    for part in range(1, CHUNKS):
        share(part)
    wait_sent(out_a, a_send, 0)
    wait_first(go_send)
    wait_second(go_send)
    wait_for(go_buf.at[1], go_recv.at[4])
    wait_for(go_buf.at[0], go_send.at[4])
    for chunk in range(CHUNKS):
        arrived(4, chunk, 1 if chunk < CHUNKS // 2 else -1)

    acc = jnp.zeros((256, 256), jnp.float32)
    for m in range(HALF):
        lhs = jnp.concatenate(
            [a_buf[:, 2 * m].reshape(256, 128), a_buf[:, 2 * m + 1].reshape(256, 128)], axis=1
        )
        rhs = jnp.concatenate([go_buf[0, m // 4, m % 4], go_buf[1, m // 4, m % 4]], axis=0)
        acc = acc + jnp.dot(lhs, rhs, preferred_element_type=jnp.float32)
    for c in range(2):
        pieces[:, c] = acc[:, c * 128 : (c + 1) * 128].reshape(16, 16, 128)

    keep(pieces.at[me // 2, odd], gbox.at[me], g_recv, 0)
    to_plane(1, N_DP, lambda peer: send(
        pieces.at[peer // 2, lax.rem(peer, 2)], gbox.at[me], g_send, g_recv, 0, peer
    ))

    def fill(o):
        for s in range(2):
            index = table_s[0, 2 * o + s]
            used = jnp.maximum(index, 0)
            value = pieces[used // 2, lax.rem(used, 2)]
            outbox[o, s] = jnp.where(index >= 0, value, 0.0)

    def to_owner(peer):
        fill(peer)
        send(outbox.at[peer], inbox.at[me], d_send, d_recv, 0, peer)

    to_plane(1, N_DP, to_owner)
    fill(me)
    keep(outbox.at[me], inbox.at[me], d_recv, 0)

    wait_for(uq, p_recv.at[1])
    second = lax.rem(table_s[1, me], 2) == 1
    for a in range(4):
        for i in range(3):
            b = (a + i) % 4
            codes = uq[b * 8, 48:64].astype(jnp.int32)
            unit = unit_of(jnp.where(second, codes[10:11], codes[8:9]))
            level = uq[a * 8 : a * 8 + 8, i * 16 : i * 16 + 16].reshape(128, 128)
            level = level.astype(jnp.int32).astype(jnp.float32) * unit
            old_left[a * 128 : a * 128 + 128, b * 128 : b * 128 + 128] = level
            if i == 1:
                old_left[b * 128 : b * 128 + 128, a * 128 : a * 128 + 128] = level.T
    codes = uq[0, 48:64].astype(jnp.int32)
    unit = unit_of(jnp.where(second, codes[14:15], codes[12:13]))
    for j in range(N_DP):
        level = uq[j, 48:64].astype(jnp.int32)
        level = jnp.where(second, level[4:8], level[0:4])
        old_right[4 * j : 4 * j + 4] = level.astype(jnp.float32) * unit
    wait_sent(sq, p_send, 0)
    wait_sent(tq, p_send, 1)
    for step in range(1, 5):
        for chunk in range(CHUNKS):
            for way in (1, -1):
                if has(step, chunk, way):
                    ring(step, chunk, way).wait_send()

    wait_for(gbox, g_recv.at[0])
    g = gbox[...].reshape(512, 128)
    gs = split(g)
    shaped = precondition(
        g,
        old_left[...] + mul(gs, gs, ((1,), (1,))),
        old_right[...] + mul(gs, gs, ((0,), (0,))),
    )
    for half in range(2):
        half_v[half] = shaped[half * 256 : (half + 1) * 256]
    send(half_v.at[1 - odd], up_box.at[odd], x_send, x_recv, 0, partner)
    keep(half_v.at[odd], up_box.at[odd], x_recv, 1)

    wait_for(inbox, d_recv.at[0])
    for s in range(2):
        gs = split(inbox[:, s].reshape(512, 128))
        nl_out[0, s] = decay_rate * left_v[s] + mul(gs, gs, ((1,), (1,)))
        nr_out[0, s] = decay_rate * right_v[s] + mul(gs, gs, ((0,), (0,)))

    wait_for(pieces.at[pl.ds(0, 15)], g_send.at[0])
    wait_for(pieces.at[15, 0], g_send.at[0])
    wait_sent(outbox, d_send, 0)
    wait_for(half_v.at[0], x_send.at[0])
    wait_for(up_box.at[0], x_recv.at[0])
    wait_for(up_box.at[0], x_recv.at[1])


def export(nl, nr, box, nl_hbm, nr_hbm, up_hbm, sem):
    pairs = [
        (nl.at[0, 0], nl_hbm.at[0, 0]),
        (nl.at[0, 1], nl_hbm.at[0, 1]),
        (nr, nr_hbm),
        (box.at[0], up_hbm.at[:, pl.ds(0, 128)]),
        (box.at[1], up_hbm.at[:, pl.ds(128, 128)]),
    ]
    copies = [pltpu.make_async_copy(src, dst, sem.at[i]) for i, (src, dst) in enumerate(pairs)]
    for copy in copies:
        copy.start()
    for copy in copies:
        copy.wait()


def on_device(acts, grad_out, owners, left_stats, right_stats):
    f32, bf16, i16, i32 = jnp.float32, jnp.bfloat16, jnp.int16, jnp.int32
    dma = pltpu.SemaphoreType.DMA
    vmem = pl.BlockSpec(memory_space=pltpu.VMEM)
    hbm = pl.BlockSpec(memory_space=pl.ANY)
    far = pl.BlockSpec(memory_space=pltpu.HBM)
    left_out = jax.ShapeDtypeStruct(left_stats.shape, f32)
    right_out = jax.ShapeDtypeStruct(right_stats.shape, f32)
    results = pl.pallas_call(
        kernel,
        name="shampoo",
        out_shape=(left_out, right_out, jax.ShapeDtypeStruct((2, 256, 128), f32)),
        in_specs=[far, far, far, far, far],
        out_specs=(vmem, vmem, hbm),
        scratch_shapes=[
            pltpu.SMEM((2, 16), i32),
            pltpu.VMEM((8, 128), i32),
            pltpu.SMEM((8, 128), i32),
            pltpu.VMEM((128, 1024), bf16),
            pltpu.VMEM((N_DP, 32, 128), bf16),
            pltpu.VMEM((N_Z, N_DP, 32, 128), bf16),
            pltpu.VMEM((2, 4, 4, 128, 256), bf16),
            pltpu.VMEM((2, 512, 512), f32),
            pltpu.VMEM((2, 128, 128), f32),
            pltpu.VMEM((N_DP, 7, 16, 128), i16),
            pltpu.VMEM((N_DP, 7, 16, 128), i16),
            pltpu.VMEM((N_DP, 64, 128), i16),
            pltpu.VMEM((N_DP, 64, 128), i16),
            pltpu.VMEM((512, 512), f32),
            pltpu.VMEM((128, 128), f32),
            pltpu.VMEM((16, 2, 16, 128), f32),
            pltpu.VMEM((N_DP, 16, 128), f32),
            pltpu.VMEM((N_DP, 2, 16, 128), f32),
            pltpu.VMEM((N_DP, 2, 16, 128), f32),
            pltpu.VMEM((2, 256, 128), f32),
            dma((6,)),
            dma((1,)), dma((CHUNKS,)),
            dma((5,)), dma((5,)),
            dma((4, CHUNKS)), dma((4, CHUNKS)), dma((4, CHUNKS)), dma((4, CHUNKS)),
            dma((2,)), dma((2,)),
            dma((1,)), dma((1,)),
            dma((1,)), dma((1,)),
            dma((1,)), dma((2,)),
        ],
        compiler_params=pltpu.CompilerParams(
            collective_id=0, has_side_effects=True, vmem_limit_bytes=32 << 20
        ),
    )(*(pltpu.with_memory_space_constraint(x, pltpu.HBM) for x in (
        owners.T, acts, grad_out, left_stats, right_stats
    )))
    return pl.pallas_call(
        export,
        name="export",
        out_shape=(left_out, right_out, jax.ShapeDtypeStruct((256, 256), f32)),
        in_specs=[hbm, hbm, hbm],
        out_specs=(far, far, far),
        scratch_shapes=[dma((5,))],
        compiler_params=pltpu.CompilerParams(vmem_limit_bytes=16 << 20),
    )(*results)


def solution(mesh):
    in_specs = (
        P("dp", ("tensor", "pre")),
        P("dp", ("tensor", "pre")),
        P(None, ("tensor", "pre")),
        P("dp", None, None, ("tensor", "pre")),
        P("dp", None, None, ("tensor", "pre")),
    )
    out_specs = (
        P("dp", None, None, ("tensor", "pre")),
        P("dp", None, None, ("tensor", "pre")),
        P("dp", ("tensor", "pre")),
    )
    return jax.shard_map(
        on_device, mesh=mesh, in_specs=in_specs, out_specs=out_specs, check_vma=False
    )
```

```python
import math

import jax
import jax.numpy as jnp
from jax import lax
from jax.experimental import pallas as pl
from jax.experimental.pallas import tpu as pltpu
from jax.sharding import PartitionSpec as P

MESH = pl.DeviceIdType.MESH
N_DP = 32
HALF = 16
N_Z = 8
CHUNKS = 4
PER = N_DP // CHUNKS
LEVELS = 32760.0
decay_rate = 0.95
graft_eps = 1e-06


def split(x):
    hi = x.astype(jnp.bfloat16)
    lo = (x - hi.astype(jnp.float32)).astype(jnp.bfloat16)
    return hi, lo


def dot(a, b, dims):
    return lax.dot_general(a, b, (dims, ((), ())), preferred_element_type=jnp.float32)


def mul(a, b, dims=((1,), (0,))):
    return dot(a[0], b[0], dims) + (dot(a[0], b[1], dims) + dot(a[1], b[0], dims))


def eye_of(n):
    rows = lax.broadcasted_iota(jnp.int32, (n, n), 0)
    cols = lax.broadcasted_iota(jnp.int32, (n, n), 1)
    return jnp.where(rows == cols, 1.25, 0.0).astype(jnp.float32)


def total(x):
    return jnp.sum(jnp.sum(x, axis=0, keepdims=True), axis=1, keepdims=True)


def right_steps(right, z_r, out):
    eye = eye_of(128)

    def first():
        n = z_r * right
        out["n"] = split(n)
        out["f1"] = split(eye - 0.25 * n)
        out["s"] = split(mul(out["f1"], out["f1"]))

    def fourth():
        out["q"] = split(mul(out["s"], out["s"]))

    def second():
        n = mul(out["q"], out["n"])
        out["n"] = split(n)
        out["f2"] = split(eye - 0.25 * n)

    def both():
        out["f12"] = split(mul(out["f1"], out["f2"]))
        out["s"] = split(mul(out["f2"], out["f2"]))

    def third():
        out["f3"] = split(eye - 0.25 * mul(out["q"], out["n"]))

    def last():
        out["root"] = split(mul(out["f12"], out["f3"]))

    return [first, fourth, second, both, fourth, third, last]


def precondition(g, left, right):
    eye = eye_of(512)
    z_l = 2.5 * lax.rsqrt(total(left * left))
    z_r = 2.5 * lax.rsqrt(total(right * right))
    made = {}
    steps = right_steps(right, z_r, made)

    def step():
        if steps:
            steps.pop(0)()

    m = z_l * left
    ms = split(m)
    fs = split(eye - 0.25 * m)
    step()
    gt = g.T
    ss = split(mul(fs, fs))
    step()
    v1 = 1.25 * gt - 0.25 * mul(split(gt), ms)
    qs = split(mul(ss, ss))
    step()
    m2s = split(mul(qs, ms))
    step()
    v2 = 1.25 * v1 - 0.25 * mul(split(v1), m2s)
    step()
    w = mul(split(v2), m2s)
    step()
    for _ in range(4):
        w = 1.25 * w - 0.25 * mul(split(w), m2s)
        step()
    v3 = 1.25 * v2 - 0.25 * w
    shaped = mul(made["root"], split(v3)).T
    shaped = shaped * (jnp.sqrt(jnp.sqrt(z_l)) * jnp.sqrt(jnp.sqrt(z_r)))
    count = 1.0 / (512 * 128)
    grad_mean = total(g * g) * count
    shaped_mean = total(shaped * shaped) * count
    return shaped * jnp.sqrt(grad_mean / (shaped_mean + graft_eps))


def tables(owners):
    shape = (N_DP, 128)
    sub = lax.broadcasted_iota(jnp.int32, shape, 0)
    lane = lax.broadcasted_iota(jnp.int32, shape, 1)
    across = jnp.full(shape, -1, jnp.int32)
    down = jnp.zeros(shape, jnp.int32)
    for k in range(N_DP):
        owner = owners[k % 2, k // 2]
        across = jnp.where(lane == k, owner, across)
        down = jnp.where(sub == k, owner, down)
    same = across == down
    place = 2 * across[:1] + jnp.sum(
        jnp.where(same & (sub < lane), 1, 0), axis=0, keepdims=True
    )
    place_down = 2 * down + jnp.sum(jnp.where(same & (lane < sub), 1, 0), axis=1, keepdims=True)
    block = jnp.sum(jnp.where(place_down == lane, sub + 1, 0), axis=0, keepdims=True) - 1
    return block, place


def scale_of(stats):
    top = jnp.maximum(jnp.max(stats, axis=0, keepdims=True), 1e-30)
    code = jnp.ceil(jnp.log(top) * (256.0 / math.log(2.0)))
    return code.astype(jnp.int32), LEVELS * jnp.exp2(code * (-1.0 / 256.0))


def unit_of(code):
    return (decay_rate / LEVELS) * jnp.exp2(code.astype(jnp.float32) * (1.0 / 256.0))


def kernel(
    owners_hbm, acts_hbm, go_hbm, left_hbm, right_hbm,
    nl_out, nr_out, up_box,
    owners_s, table_v, table_s, acts_v, out_a, a_buf, go_buf, left_v, right_v,
    sq, rq, tq, uq, old_left, old_right, pieces, gbox, outbox, inbox, half_v,
    in_sem, a_send, a_recv, go_send, go_recv,
    zr_send, zr_recv, zl_send, zl_recv,
    p_send, p_recv, g_send, g_recv, d_send, d_recv, x_send, x_recv,
):
    me = lax.axis_index("dp")
    tensor = lax.axis_index("tensor")
    pre = lax.axis_index("pre")
    z = pre * 4 + tensor
    odd = lax.rem(me, 2)
    partner = me + 1 - 2 * odd
    column = me // PER
    own = lax.rem(me, PER) // 2

    load_owners = pltpu.make_async_copy(owners_hbm, owners_s, in_sem.at[4])
    load_owners.start()
    load_acts = pltpu.make_async_copy(acts_hbm, acts_v, in_sem.at[0])
    load_acts.start()
    load_left = pltpu.make_async_copy(left_hbm.at[0], left_v, in_sem.at[2])
    load_left.start()
    load_right = pltpu.make_async_copy(right_hbm.at[0], right_v, in_sem.at[3])
    load_right.start()
    load_go = pltpu.make_async_copy(go_hbm, go_buf.at[odd, 0, own], in_sem.at[1])
    load_go.start()

    def z_dev(zz):
        zz = lax.rem(zz + N_Z, N_Z)
        return {"tensor": lax.rem(zz, 4), "pre": zz // 4}

    def slice_of(zz):
        zz = lax.rem(zz + N_Z, N_Z)
        return lax.rem(zz, 4) * 2 + zz // 4

    def wait_for(ref, sem):
        pltpu.make_async_copy(ref, ref, sem).wait()

    def to_plane(begin, end, make):
        def one(i, carry):
            make(lax.rem(me + i, N_DP))
            return carry

        lax.fori_loop(max(begin, 1), end, one, 0)

    def send(src, dst, sends, recvs, k, peer):
        pltpu.make_async_remote_copy(
            src_ref=src, dst_ref=dst, send_sem=sends.at[k], recv_sem=recvs.at[k],
            device_id={"dp": peer}, device_id_type=MESH,
        ).start()

    def keep(src, dst, recvs, k):
        pltpu.make_async_copy(src, dst, recvs.at[k]).start()

    def wait_sent(box, sends, k):
        wait_for(box.at[pl.ds(0, N_DP - 1)], sends.at[k])

    barrier = pltpu.get_barrier_semaphore()

    def greet(i, carry):
        pl.semaphore_signal(
            barrier, inc=1, device_id={"dp": lax.rem(me + i, N_DP)}, device_id_type=MESH
        )
        return carry

    lax.fori_loop(1, N_DP, greet, 0)
    for step in (1, -1):
        pl.semaphore_signal(barrier, inc=1, device_id=z_dev(z + step), device_id_type=MESH)

    mine = slice_of(z)
    load_acts.wait()
    for hop in range(CHUNKS):
        goal = lax.rem(column + hop, CHUNKS)
        for part in range(2):
            start = pl.multiple_of((goal + part * CHUNKS) * 128, 128)
            turned = acts_v[:, pl.ds(start, 128)].T
            for e in range(PER):
                out_a[goal * PER + e, part * 16 : part * 16 + 16] = turned[e * 16 : e * 16 + 16]
        if hop == 0:
            pltpu.make_async_copy(
                out_a.at[me], a_buf.at[mine, lax.rem(me, PER)], a_recv.at[0]
            ).start()
            pl.semaphore_wait(barrier, N_DP + 1)

        def send_a(i, carry):
            peer = goal * PER + lax.rem(me + i, PER)
            pltpu.make_async_remote_copy(
                src_ref=out_a.at[peer], dst_ref=a_buf.at[mine, hop * PER + lax.rem(me, PER)],
                send_sem=a_send.at[0], recv_sem=a_recv.at[hop],
                device_id={"dp": peer}, device_id_type=MESH,
            ).start()
            return carry

        lax.fori_loop(1 if hop == 0 else 0, PER, send_a, 0)

    def x_peer(hop):
        return lax.rem(column + hop, CHUNKS) * PER + lax.rem(me, PER)

    def y_peer(hop):
        return column * PER + lax.rem(me + 2 * hop, PER)

    def first_stage(hop):
        near = go_buf.at[odd, 0, own, pl.ds(0, 64)]
        far = go_buf.at[odd, 0, own, pl.ds(64, 64)]
        send(near, go_buf.at[odd, hop, own, pl.ds(0, 64)], go_send, go_recv, 0, x_peer(hop))
        send(far, far, go_send, go_recv, 1, y_peer(hop))

    def second_stage(hop):
        near = go_buf.at[odd, :, own, pl.ds(0, 64)]
        far = go_buf.at[odd, 0, :, pl.ds(64, 64)]
        send(near, near, go_send, go_recv, 2, y_peer(hop))
        send(far, go_buf.at[odd, hop, :, pl.ds(64, 64)], go_send, go_recv, 3, x_peer(hop))

    def wait_first(sems):
        for k in (0, 1):
            wait_for(go_buf.at[0, 0, pl.ds(0, 3), pl.ds(0, 64)], sems.at[k])

    def wait_second(sems):
        for k in (2, 3):
            wait_for(go_buf.at[0, pl.ds(0, 3), :, pl.ds(0, 64)], sems.at[k])

    def send_old(peer):
        send(sq.at[peer], rq.at[me], p_send, p_recv, 0, peer)

    def take_share(k):
        where = table_s[1, k]
        for i in range(3):
            tq[k, i * 16 : i * 16 + 16] = rq[where // 2, lax.rem(where, 2) * 3 + i]
        tq[k, 48:64] = rq[where // 2, 6]

    def send_share(peer):
        take_share(peer)
        send(tq.at[peer], uq.at[me], p_send, p_recv, 1, peer)

    def ring(step, chunk, way):
        sems = (zr_send, zr_recv) if way == 1 else (zl_send, zl_recv)
        ref = a_buf.at[slice_of(z - way * (step - 1)), pl.ds(chunk * PER, PER)]
        return pltpu.make_async_remote_copy(
            src_ref=ref, dst_ref=ref,
            send_sem=sems[0].at[step - 1, chunk], recv_sem=sems[1].at[step - 1, chunk],
            device_id=z_dev(z + way), device_id_type=MESH,
        )

    def arrived(step, chunk, way):
        sems = zr_recv if way == 1 else zl_recv
        wait_for(a_buf.at[slice_of(z - way * step), pl.ds(chunk * PER, PER)], sems.at[step - 1, chunk])

    def has(step, chunk, way):
        return step < 4 or (chunk < CHUNKS // 2) == (way == 1)

    codes_l = []

    def level_left(s):
        if s == 0:
            load_left.wait()
        code, scale = scale_of(left_v[s])
        codes_l.append(code)
        for a in range(4):
            for i in range(3):
                b = (a + i) % 4
                level = left_v[s, a * 128 : a * 128 + 128, b * 128 : b * 128 + 128]
                level = jnp.round(level * scale[:, b * 128 : b * 128 + 128])
                level = level.astype(jnp.int32).astype(jnp.int16)
                sq[a * 8 : a * 8 + 8, s * 3 + i] = level.reshape(8, 16, 128)

    def level_right():
        load_right.wait()
        row = lax.broadcasted_iota(jnp.int32, (8, 128), 0)
        rights, codes_r = [], []
        for s in range(2):
            code, scale = scale_of(right_v[s])
            codes_r.append(code)
            rights.append(jnp.round(right_v[s] * scale).astype(jnp.int32))
        for a in range(4):
            codes = [c[:, a * 128 : a * 128 + 128] for c in codes_l] + codes_r
            low = jnp.where(
                row < 4,
                jnp.where(row < 2, codes[0], codes[1]),
                jnp.where(row < 6, codes[2], codes[3]),
            )
            for j in range(8 * a, 8 * a + 8):
                high = jnp.concatenate([r[4 * j : 4 * j + 4] for r in rights], axis=0)
                sq[j, 6] = jnp.concatenate([high, low], axis=0).astype(jnp.int16)
        keep(sq.at[me], rq.at[me], p_recv, 0)

    def make_tables():
        load_owners.wait()
        block, place = tables(owners_s)
        table_v[0:1] = block
        table_v[1:2] = place
        load_table.start()

    def old(part):
        to_plane(part * PER, (part + 1) * PER, send_old)

    def share(part):
        if part == 0:
            load_table.wait()
            wait_for(rq, p_recv.at[0])
            take_share(me)
            keep(tq.at[me], uq.at[me], p_recv, 1)
        to_plane(part * PER, (part + 1) * PER, send_share)

    load_table = pltpu.make_async_copy(table_v, table_s, in_sem.at[5])
    plan = {
        (1, 0): [load_go.wait, lambda: first_stage(1), lambda: level_left(0)],
        (1, 1): [lambda: first_stage(2), lambda: level_left(1)],
        (1, 2): [lambda: first_stage(3), level_right],
        (1, 3): [lambda: old(0), lambda: old(1)],
        (2, 0): [lambda: old(2), lambda: old(3)],
        (2, 1): [make_tables],
        (2, 2): [lambda: wait_first(go_recv), lambda: second_stage(1)],
        (2, 3): [lambda: second_stage(2)],
        (3, 0): [lambda: second_stage(3)],
        (4, 0): [lambda: share(0)],
    }
    for step in range(1, 5):
        for chunk in range(CHUNKS):
            if step == 1:
                wait_for(a_buf.at[mine, pl.ds(chunk * PER, PER)], a_recv.at[chunk])
            for way in (1, -1):
                if step > 1:
                    arrived(step - 1, chunk, way)
                if has(step, chunk, way):
                    ring(step, chunk, way).start()
            for act in plan.get((step, chunk), ()):
                act()

    wait_second(go_recv)
    send(go_buf.at[odd], go_buf.at[odd], go_send, go_recv, 4, partner)
    for part in range(1, CHUNKS):
        share(part)
    wait_sent(out_a, a_send, 0)
    wait_first(go_send)
    wait_second(go_send)
    wait_for(go_buf.at[1], go_recv.at[4])
    wait_for(go_buf.at[0], go_send.at[4])
    for chunk in range(CHUNKS):
        arrived(4, chunk, 1 if chunk < CHUNKS // 2 else -1)

    acc = jnp.zeros((256, 256), jnp.float32)
    for m in range(HALF):
        lhs = jnp.concatenate(
            [a_buf[:, 2 * m].reshape(256, 128), a_buf[:, 2 * m + 1].reshape(256, 128)], axis=1
        )
        rhs = jnp.concatenate([go_buf[0, m // 4, m % 4], go_buf[1, m // 4, m % 4]], axis=0)
        acc = acc + jnp.dot(lhs, rhs, preferred_element_type=jnp.float32)
    for c in range(2):
        pieces[:, c] = acc[:, c * 128 : (c + 1) * 128].reshape(16, 16, 128)

    keep(pieces.at[me // 2, odd], gbox.at[me], g_recv, 0)
    to_plane(1, N_DP, lambda peer: send(
        pieces.at[peer // 2, lax.rem(peer, 2)], gbox.at[me], g_send, g_recv, 0, peer
    ))

    def fill(o):
        for s in range(2):
            index = table_s[0, 2 * o + s]
            used = jnp.maximum(index, 0)
            value = pieces[used // 2, lax.rem(used, 2)]
            outbox[o, s] = jnp.where(index >= 0, value, 0.0)

    def to_owner(peer):
        fill(peer)
        send(outbox.at[peer], inbox.at[me], d_send, d_recv, 0, peer)

    to_plane(1, N_DP, to_owner)
    fill(me)
    keep(outbox.at[me], inbox.at[me], d_recv, 0)

    wait_for(uq, p_recv.at[1])
    second = lax.rem(table_s[1, me], 2) == 1
    for a in range(4):
        for i in range(3):
            b = (a + i) % 4
            codes = uq[b * 8, 48:64].astype(jnp.int32)
            unit = unit_of(jnp.where(second, codes[10:11], codes[8:9]))
            level = uq[a * 8 : a * 8 + 8, i * 16 : i * 16 + 16].reshape(128, 128)
            level = level.astype(jnp.int32).astype(jnp.float32) * unit
            old_left[a * 128 : a * 128 + 128, b * 128 : b * 128 + 128] = level
            if i == 1:
                old_left[b * 128 : b * 128 + 128, a * 128 : a * 128 + 128] = level.T
    codes = uq[0, 48:64].astype(jnp.int32)
    unit = unit_of(jnp.where(second, codes[14:15], codes[12:13]))
    for j in range(N_DP):
        level = uq[j, 48:64].astype(jnp.int32)
        level = jnp.where(second, level[4:8], level[0:4])
        old_right[4 * j : 4 * j + 4] = level.astype(jnp.float32) * unit
    wait_sent(sq, p_send, 0)
    wait_sent(tq, p_send, 1)
    for step in range(1, 5):
        for chunk in range(CHUNKS):
            for way in (1, -1):
                if has(step, chunk, way):
                    ring(step, chunk, way).wait_send()

    wait_for(gbox, g_recv.at[0])
    g = gbox[...].reshape(512, 128)
    gs = split(g)
    shaped = precondition(
        g,
        old_left[...] + mul(gs, gs, ((1,), (1,))),
        old_right[...] + mul(gs, gs, ((0,), (0,))),
    )
    for half in range(2):
        half_v[half] = shaped[half * 256 : (half + 1) * 256]
    send(half_v.at[1 - odd], up_box.at[odd], x_send, x_recv, 0, partner)
    keep(half_v.at[odd], up_box.at[odd], x_recv, 1)

    wait_for(inbox, d_recv.at[0])
    for s in range(2):
        gs = split(inbox[:, s].reshape(512, 128))
        nl_out[0, s] = decay_rate * left_v[s] + mul(gs, gs, ((1,), (1,)))
        nr_out[0, s] = decay_rate * right_v[s] + mul(gs, gs, ((0,), (0,)))

    wait_for(pieces.at[pl.ds(0, 15)], g_send.at[0])
    wait_for(pieces.at[15, 0], g_send.at[0])
    wait_sent(outbox, d_send, 0)
    wait_for(half_v.at[0], x_send.at[0])
    wait_for(up_box.at[0], x_recv.at[0])
    wait_for(up_box.at[0], x_recv.at[1])


def export(nl, nr, box, nl_hbm, nr_hbm, up_hbm, sem):
    pairs = [
        (nl.at[0, 0], nl_hbm.at[0, 0]),
        (nl.at[0, 1], nl_hbm.at[0, 1]),
        (nr, nr_hbm),
        (box.at[0], up_hbm.at[:, pl.ds(0, 128)]),
        (box.at[1], up_hbm.at[:, pl.ds(128, 128)]),
    ]
    copies = [pltpu.make_async_copy(src, dst, sem.at[i]) for i, (src, dst) in enumerate(pairs)]
    for copy in copies:
        copy.start()
    for copy in copies:
        copy.wait()


def on_device(acts, grad_out, owners, left_stats, right_stats):
    f32, bf16, i16, i32 = jnp.float32, jnp.bfloat16, jnp.int16, jnp.int32
    dma = pltpu.SemaphoreType.DMA
    vmem = pl.BlockSpec(memory_space=pltpu.VMEM)
    hbm = pl.BlockSpec(memory_space=pl.ANY)
    far = pl.BlockSpec(memory_space=pltpu.HBM)
    left_out = jax.ShapeDtypeStruct(left_stats.shape, f32)
    right_out = jax.ShapeDtypeStruct(right_stats.shape, f32)
    results = pl.pallas_call(
        kernel,
        name="shampoo",
        out_shape=(left_out, right_out, jax.ShapeDtypeStruct((2, 256, 128), f32)),
        in_specs=[far, far, far, far, far],
        out_specs=(vmem, vmem, hbm),
        scratch_shapes=[
            pltpu.SMEM((2, 16), i32),
            pltpu.VMEM((8, 128), i32),
            pltpu.SMEM((8, 128), i32),
            pltpu.VMEM((128, 1024), bf16),
            pltpu.VMEM((N_DP, 32, 128), bf16),
            pltpu.VMEM((N_Z, N_DP, 32, 128), bf16),
            pltpu.VMEM((2, 4, 4, 128, 256), bf16),
            pltpu.VMEM((2, 512, 512), f32),
            pltpu.VMEM((2, 128, 128), f32),
            pltpu.VMEM((N_DP, 7, 16, 128), i16),
            pltpu.VMEM((N_DP, 7, 16, 128), i16),
            pltpu.VMEM((N_DP, 64, 128), i16),
            pltpu.VMEM((N_DP, 64, 128), i16),
            pltpu.VMEM((512, 512), f32),
            pltpu.VMEM((128, 128), f32),
            pltpu.VMEM((16, 2, 16, 128), f32),
            pltpu.VMEM((N_DP, 16, 128), f32),
            pltpu.VMEM((N_DP, 2, 16, 128), f32),
            pltpu.VMEM((N_DP, 2, 16, 128), f32),
            pltpu.VMEM((2, 256, 128), f32),
            dma((6,)),
            dma((1,)), dma((CHUNKS,)),
            dma((5,)), dma((5,)),
            dma((4, CHUNKS)), dma((4, CHUNKS)), dma((4, CHUNKS)), dma((4, CHUNKS)),
            dma((2,)), dma((2,)),
            dma((1,)), dma((1,)),
            dma((1,)), dma((1,)),
            dma((1,)), dma((2,)),
        ],
        compiler_params=pltpu.CompilerParams(
            collective_id=0, has_side_effects=True, vmem_limit_bytes=32 << 20
        ),
    )(*(pltpu.with_memory_space_constraint(x, pltpu.HBM) for x in (
        owners.T, acts, grad_out, left_stats, right_stats
    )))
    return pl.pallas_call(
        export,
        name="export",
        out_shape=(left_out, right_out, jax.ShapeDtypeStruct((256, 256), f32)),
        in_specs=[hbm, hbm, hbm],
        out_specs=(far, far, far),
        scratch_shapes=[dma((5,))],
        compiler_params=pltpu.CompilerParams(vmem_limit_bytes=16 << 20),
    )(*results)


def solution(mesh):
    in_specs = (
        P("dp", ("tensor", "pre")),
        P("dp", ("tensor", "pre")),
        P(None, ("tensor", "pre")),
        P("dp", None, None, ("tensor", "pre")),
        P("dp", None, None, ("tensor", "pre")),
    )
    out_specs = (
        P("dp", None, None, ("tensor", "pre")),
        P("dp", None, None, ("tensor", "pre")),
        P("dp", ("tensor", "pre")),
    )
    return jax.shard_map(
        on_device, mesh=mesh, in_specs=in_specs, out_specs=out_specs, check_vma=False
    )
```
